256 devices in a mesh: dp: 32 (over z, x_lo, core), seg: 8 (over x_hi, y).
Axes of the slice: x: 4 (x_hi: 2, x_lo: 2; x = x_hi * 2 + x_lo), y: 4, z: 8, core: 2. Of those that a mesh axis runs over, the one named last changes fastest.
Arguments:
- tokens: bfloat16 [32, 1024, 768], P('dp', 'seg'), may hold values from -6 to 6
- coords: int32 [32, 1024, 2], P('dp', 'seg'), may hold values from 0 to 255
- lengths: int32 [32], P('dp'), may hold values from 256 to 1024, as said below
- w_qkv: bfloat16 [768, 2304], replicated, may hold values from -16 to 16
- w_out: bfloat16 [768, 768], replicated, may hold values from -1.5 to 1.5
- cotangent: bfloat16 [32, 1024, 768], P('dp', 'seg'), may hold values from -6 to 6
Outputs:
- layer_out: bfloat16 [32, 1024, 768], P('dp', 'seg')
- token_grad: bfloat16 [32, 1024, 768], P('dp', 'seg')
- grad_w_qkv: float32 [768, 2304], P('seg', 'dp')
- grad_w_out: float32 [768, 768], P('seg', 'dp')
The draws below stay inside these ranges and needn't reach their ends.
Inputs may be any that keep to these rules, and one draw needn't show every extreme that they name: `lengths`: each slide's length lies in the range; in every draw one slide has exactly 1024 tiles and another exactly 256.
All inputs are finite; a program needn't handle non-finite values.
Results may differ from the reference program's by a relative error of at most 0.034.
Values may be sent and summed in bfloat16 or wider, within the bound.
No kernel may reach another device: no remote copies, remote signals or barrier semaphores. Data moves between devices by JAX's collectives and lax.ppermute only.
A program may use at most 64 MiB of HBM per device.

```python
import jax
import jax.numpy as jnp
from jax import lax

D = 768
HEADS = 16
TOK_DEV = 128
RATE = 4
GRID = 256
SLIDES = 32
SEQ = 1024
N_SEG = 8


def draw_lengths(key, part):
    key = jax.random.fold_in(key, 11)
    first_key, second_key, third_key = jax.random.split(key, 3)
    base = jax.random.randint(first_key, (SLIDES,), SEQ // 4, SEQ + 1)
    longest = jax.random.randint(second_key, (), 0, SLIDES)
    shortest = (longest + 1 + jax.random.randint(third_key, (), 0, SLIDES - 1)) % SLIDES
    index = jnp.arange(SLIDES)
    result = jnp.where(index == longest, SEQ, jnp.where(index == shortest, SEQ // 4, base))
    return result.astype(jnp.int32)


def draw_w_qkv(key, part):
    key = jax.random.fold_in(key, 23)
    first_key = jax.random.fold_in(key, 0)
    base = jax.random.truncated_normal(first_key, -4.0, 4.0, (D, 3 * D), jnp.float32) * D ** (-0.5)
    return base.astype(jnp.bfloat16)


def place_ends(entries, rng, least, largest):
    shape = entries.shape
    spot = [jax.random.randint(jax.random.fold_in(rng, axis), (), 0, shape[axis]) for axis in range(len(shape))]
    entries = entries.at[tuple(spot)].set(least)
    longest = shape.index(max(shape))
    spot[longest] = (spot[longest] + 1) % shape[longest]
    return entries.at[tuple(spot)].set(largest)


def block_scale(own_key, dims, pieces, smallest, high):
    loudness, own = 1.0, jax.random.fold_in(own_key, 6)
    for dim, shards_of in pieces:
        steps = jnp.exp(jax.random.uniform(jax.random.fold_in(own, dim), (shards_of,), jnp.float32, smallest / len(pieces), high / len(pieces)))
        loudness = loudness * jnp.repeat(steps, dims[dim] // shards_of).reshape([-1 if axis == dim else 1 for axis in range(len(dims))])
    return loudness


def bell_draw(rng, extent, scale, reach, pieces=(), kind=jnp.bfloat16):
    entries = jax.random.normal(rng, extent, jnp.float32) * scale
    if len(pieces) > 0:
        entries = block_scale(rng, extent, pieces, -0.22, 0.18) * entries
    return jnp.clip(entries, min=-reach, max=reach).astype(kind)


def setup_inputs(seed: int = 0) -> dict:
    arg_keys = jax.random.split(jax.random.key(seed), 7)
    return {
        "tokens": bell_draw(arg_keys[0], (SLIDES, SEQ, D), 1.0, 6.0, ((0, 32), (1, 8))),
        "coords": place_ends(jax.random.randint(arg_keys[1], (SLIDES, SEQ, 2), 0, GRID), jax.random.fold_in(arg_keys[1], 1), 0, GRID - 1).astype(jnp.int32),
        "lengths": draw_lengths(jax.random.fold_in(arg_keys[6], 71), 0),
        "w_qkv": draw_w_qkv(jax.random.fold_in(arg_keys[6], 71), 0),
        "w_out": bell_draw(arg_keys[4], (D, D), HEADS ** -0.5, 1.5),
        "cotangent": bell_draw(arg_keys[5], (SLIDES, SEQ, D), 1.0, 6.0, ((0, 32), (1, 8))),
    }


EPSILON = 1e-05
NEG_FILL = -1e+30

def position_code(coords, width):
    quarter = width // 4
    freqs = jnp.exp(-jnp.log(10000.0) * jnp.arange(quarter, dtype=jnp.float32) / quarter)
    across = coords[:, 0:1].astype(jnp.float32) * freqs[None, :]
    upward = coords[:, 1:2].astype(jnp.float32) * freqs[None, :]
    return jnp.concatenate([jnp.sin(across), jnp.cos(across), jnp.sin(upward), jnp.cos(upward)], axis=1)

def layer_norm(embedded):
    centred = embedded - lax.optimization_barrier(jnp.mean(embedded, axis=-1, keepdims=True))
    spread = lax.optimization_barrier(jnp.mean(centred * centred, axis=-1, keepdims=True))
    return centred * lax.rsqrt(spread + EPSILON)

def project_in(tokens, coords, w_qkv):
    embedded = tokens.astype(jnp.float32) + position_code(coords, tokens.shape[-1])
    normed = layer_norm(embedded).astype(jnp.bfloat16)
    packed = jnp.dot(normed, w_qkv, preferred_element_type=jnp.float32).astype(jnp.bfloat16)
    return (embedded, normed, packed)

def project_in_back(embedded, normed, w_qkv, packed_grad):
    grad_weight = lax.dot_general(normed, packed_grad, (((0,), (0,)), ((), ())), preferred_element_type=jnp.float32)
    normed_grad = lax.dot_general(packed_grad, w_qkv, (((1,), (1,)), ((), ())), preferred_element_type=jnp.float32)
    _, norm_pull = jax.vjp(layer_norm, embedded)
    token_grad = norm_pull(normed_grad)[0].astype(jnp.bfloat16)
    return (token_grad, grad_weight)

def split_heads(packed, head_count):
    row_count = packed.shape[0]
    width = packed.shape[1] // 3
    shaped = packed.reshape(row_count, 3, head_count, width // head_count)
    return (shaped[:, 0], shaped[:, 1], shaped[:, 2])

def sample_mask(head_count, dilation):
    return jnp.arange(dilation, dtype=jnp.int32)[:, None] == (jnp.arange(head_count, dtype=jnp.int32) % dilation)[None, :]

def pick_samples(rows_in, dilation):
    grouped = rows_in.reshape((rows_in.shape[0] // dilation, dilation) + rows_in.shape[1:])
    chosen = sample_mask(rows_in.shape[1], dilation).astype(rows_in.dtype)
    chosen = chosen.reshape(chosen.shape + (1,) * (rows_in.ndim - 2))
    return lax.optimization_barrier(jnp.sum(grouped * chosen[None], axis=1))

def place_samples(samples, dilation):
    chosen = sample_mask(samples.shape[1], dilation).astype(samples.dtype)
    chosen = chosen.reshape(chosen.shape + (1,) * (samples.ndim - 2))
    spread = samples[:, None] * chosen[None]
    return spread.reshape((samples.shape[0] * dilation,) + samples.shape[1:])

def masked_softmax(scores, allowed):
    scores = jnp.where(allowed, scores, NEG_FILL)
    row_max = lax.stop_gradient(lax.optimization_barrier(jnp.max(scores, axis=-1, keepdims=True)))
    shifted = jnp.exp(scores - row_max)
    row_sum = lax.optimization_barrier(jnp.sum(shifted, axis=-1, keepdims=True))
    weights = lax.optimization_barrier((shifted / row_sum).astype(jnp.bfloat16)).astype(jnp.float32)
    return (weights, (row_max + jnp.log(row_sum))[..., 0])

def dense_branch(queries, key_rows, value_rows, positions, length):
    score_scale = queries.shape[-1] ** (-0.5)
    scores = jnp.einsum('bqhe,bkhe->bhqk', queries.astype(jnp.float32), key_rows.astype(jnp.float32)) * score_scale
    allowed = jnp.logical_or(positions[:, None, None, :] < length, positions[:, None, :, None] == positions[:, None, None, :])
    weights, log_total = masked_softmax(scores, allowed)
    output = jnp.einsum('bhqk,bkhe->bqhe', weights, value_rows.astype(jnp.float32))
    return (output, jnp.transpose(log_total, (0, 2, 1)))

def sparse_branch(queries, key_rows, value_rows, query_index, key_index, dilation, length):
    score_scale = queries.shape[-1] ** (-0.5)
    offsets = jnp.arange(queries.shape[1], dtype=jnp.int32) % dilation
    scores = jnp.einsum('qhe,khe->hqk', queries.astype(jnp.float32), key_rows) * score_scale
    key_place = key_index[None, :] * dilation + offsets[:, None]
    allowed = jnp.logical_or(key_place[:, None, :] < length, query_index[None, :, None] == key_index[None, None, :])
    weights, log_total = masked_softmax(scores, allowed)
    output = jnp.einsum('hqk,khe->qhe', weights, value_rows)
    return (output, jnp.transpose(log_total))

def combine_branches(dense_out, dense_lse, sparse_out, sparse_lse, dilation):
    sampled = jnp.tile(sample_mask(dense_lse.shape[1], dilation), (sparse_lse.shape[0], 1))
    spread_out = place_samples(sparse_out, dilation)
    spread_lse = place_samples(sparse_lse, dilation)
    larger = lax.stop_gradient(jnp.where(sampled, jnp.maximum(dense_lse, spread_lse), dense_lse))
    dense_weight = jnp.exp(dense_lse - larger)
    sparse_weight = jnp.where(sampled, jnp.exp(jnp.where(sampled, spread_lse - larger, 0.0)), 0.0)
    blended = (dense_weight[..., None] * dense_out + sparse_weight[..., None] * spread_out) / (dense_weight + sparse_weight)[..., None]
    return blended.reshape(dense_out.shape[0], -1).astype(jnp.bfloat16)

def assemble_grads(dense_grads, sparse_grads, dilation):
    query_grad = dense_grads[0] + place_samples(sparse_grads[0], dilation)
    key_grad = dense_grads[1] + place_samples(sparse_grads[1], dilation)
    value_grad = dense_grads[2] + place_samples(sparse_grads[2], dilation)
    row_count = query_grad.shape[0]
    return jnp.concatenate([query_grad.reshape(row_count, -1), key_grad.reshape(row_count, -1), value_grad.reshape(row_count, -1)], axis=1)

def project_out(blended, w_out, live):
    return jnp.where(live, jnp.dot(blended, w_out, preferred_element_type=jnp.float32), 0.0).astype(jnp.bfloat16)

def slide_pass(tokens, coords, length, w_qkv, w_out, cotangent):
    seq_len = tokens.shape[0]
    embedded, normed, packed = project_in(tokens, coords, w_qkv)
    q_rows, k_rows, v_rows = split_heads(packed, HEADS)
    positions = jnp.arange(seq_len, dtype=jnp.int32)
    block_shape = (N_SEG, TOK_DEV) + q_rows.shape[1:]

    def dense_part(q_in, k_in, v_in):
        block_out, block_lse = dense_branch(q_in.reshape(block_shape), k_in.reshape(block_shape), v_in.reshape(block_shape), positions.reshape(N_SEG, TOK_DEV), length)
        return (block_out.reshape(q_in.shape), block_lse.reshape(seq_len, -1))
    sample_index = jnp.arange(seq_len // RATE, dtype=jnp.int32)

    def sparse_part(q_in, k_in, v_in):
        return sparse_branch(q_in, k_in, v_in, sample_index, sample_index, RATE, length)

    def combine_part(first_out, first_lse, second_out, second_lse):
        return combine_branches(first_out, first_lse, second_out, second_lse, RATE)
    (dense_out, dense_lse), dense_pull = jax.vjp(dense_part, q_rows, k_rows, v_rows)
    own_keys = pick_samples(k_rows, RATE).astype(jnp.float32)
    own_values = pick_samples(v_rows, RATE).astype(jnp.float32)
    sampled_queries = pick_samples(q_rows, RATE)
    (sparse_out, sparse_lse), sparse_pull = jax.vjp(sparse_part, sampled_queries, own_keys, own_values)
    blended, combine_pull = jax.vjp(combine_part, dense_out, dense_lse, sparse_out, sparse_lse)
    live = (positions < length)[:, None]
    layer_out = project_out(blended, w_out, live)
    out_grad = jnp.where(live, cotangent, jnp.zeros_like(cotangent))
    grad_out = lax.dot_general(blended, out_grad, (((0,), (0,)), ((), ())), preferred_element_type=jnp.float32)
    blended_grad = lax.dot_general(out_grad, w_out, (((1,), (1,)), ((), ())), preferred_element_type=jnp.float32).astype(jnp.bfloat16)
    grad_dense_out, grad_dense_lse, grad_sparse_out, grad_sparse_lse = combine_pull(blended_grad)
    dense_grads = dense_pull((grad_dense_out, grad_dense_lse))
    query_sparse, key_sparse, value_sparse = sparse_pull((grad_sparse_out, grad_sparse_lse))
    sparse_grads = (query_sparse, key_sparse.astype(jnp.bfloat16), value_sparse.astype(jnp.bfloat16))
    packed_grad = assemble_grads(dense_grads, sparse_grads, RATE)
    token_grad, grad_in = project_in_back(embedded, normed, w_qkv, packed_grad)
    return (layer_out, token_grad, grad_in, grad_out)

def reference(tokens, coords, lengths, w_qkv, w_out, cotangent):

    def one_slide(running, inputs):
        layer_out, token_grad, grad_in, grad_out = slide_pass(inputs[0], inputs[1], inputs[2], w_qkv, w_out, inputs[3])
        return ((running[0] + grad_in, running[1] + grad_out), (layer_out, token_grad))
    initial = (jnp.zeros(w_qkv.shape, jnp.float32), jnp.zeros(w_out.shape, jnp.float32))
    totals, outputs = lax.scan(one_slide, initial, (tokens, coords, lengths, cotangent))
    return (outputs[0], outputs[1], totals[0], totals[1])
```

```python
import functools

import jax
import jax.numpy as jnp
from jax import lax
from jax.experimental import pallas as pl
from jax.experimental.pallas import tpu as pltpu
from jax.sharding import Mesh
from jax.sharding import PartitionSpec as P

HEADS = 16
RATE = 4
HEAD = 48
GROUP = 8
WIDE = GROUP * HEAD
ROWS = 128
SLAB = ROWS // RATE
D = 768
N_SEG = 8
BLOCK = 96
EPSILON = 1e-05
NEG_FILL = -1e30
SCALE = HEAD ** (-0.5)
BF = jnp.bfloat16
F32 = jnp.float32
VMEM = pl.BlockSpec(memory_space=pltpu.VMEM)
SMEM = pl.BlockSpec(memory_space=pltpu.SMEM)
LIMIT = 40 * 1024 * 1024


def iota(shape, dim):
    return lax.broadcasted_iota(jnp.int32, shape, dim)


def mm(a, b):
    return lax.dot_general(a, b, (((1,), (0,)), ((), ())), preferred_element_type=F32)


def mm_nt(a, b):
    return lax.dot_general(a, b, (((1,), (1,)), ((), ())), preferred_element_type=F32)


def mm_tn(a, b):
    return lax.dot_general(a, b, (((0,), (0,)), ((), ())), preferred_element_type=F32)


def regroup():
    row, col = iota((ROWS, ROWS), 0), iota((ROWS, ROWS), 1)
    return (col == RATE * (row % SLAB) + row // SLAB).astype(BF)


def place_of(row):
    return RATE * (row % SLAB) + row // SLAB


def sin_cos_code(c0, c1):
    quarter = D // 4
    col = iota((1, D), 1)
    block = col // quarter
    freqs = jnp.exp((-jnp.log(F32(10000.0))) * (col - block * quarter).astype(F32) / quarter)
    angle = jnp.where(block < 2, c0, c1) * freqs
    turns = jnp.floor(angle * F32(0.6366197723675814) + F32(0.5))
    rest = angle - turns * F32(1.5703125)
    rest = rest - turns * F32(4.837512969970703e-4)
    rest = rest - turns * F32(7.549789948768648e-8)
    sq = rest * rest
    sine = rest + rest * sq * (
        F32(-1.6666654611e-1) + sq * (F32(8.3321608736e-3) + sq * F32(-1.9515295891e-4))
    )
    cosine = (
        F32(1.0)
        - F32(0.5) * sq
        + sq * sq * (F32(4.166664568298827e-2) + sq * (F32(-1.388731625493765e-3) + sq * F32(2.443315711809948e-5)))
    )
    quadrant = turns.astype(jnp.int32) + (block & 1)
    value = jnp.where((quadrant & 1) == 1, cosine, sine)
    return jnp.where((quadrant & 2) == 2, -value, value)


def head_mask(rows_per_head):
    shape = (GROUP * rows_per_head, WIDE)
    return iota(shape, 0) // rows_per_head == iota(shape, 1) // HEAD


def split3(x):
    hi = x.astype(BF)
    rest = x - hi.astype(F32)
    mid = rest.astype(BF)
    lo = (rest - mid.astype(F32)).astype(BF)
    return hi, mid, lo


def put_scalars(base, columns):
    lane = iota(base.shape, 1)
    for n, column in enumerate(columns):
        base = jnp.where(lane == BLOCK + n, column.astype(F32), base)
    return base


def stack_slabs(array, group):
    part = array[:, group * WIDE : (group + 1) * WIDE]
    return jnp.concatenate(
        [part[SLAB * (h % RATE) : SLAB * (h % RATE) + SLAB] for h in range(GROUP)], axis=0
    )


def unstack_slabs(stack):
    return jnp.concatenate(
        [
            stack[SLAB * o : SLAB * o + SLAB] + stack[SLAB * (o + RATE) : SLAB * (o + RATE) + SLAB]
            for o in range(RATE)
        ],
        axis=0,
    )


def seg_index():
    return lax.axis_index("xh") * 4 + lax.axis_index("y")


def first_kernel(
    length_ref, tok_ref, coord_ref, cot_ref, w_qkv_ref, w_out_ref,
    message_ref, packed_ref, g_ref, xhat_ref, rstd_ref, normed_ref, grad_ref, blocks_ref,
):
    length = length_ref[0]
    base = seg_index() * ROWS
    order = regroup()
    tokens = mm(order, tok_ref[0])
    coords = mm(order, coord_ref[0].astype(F32).astype(BF))
    embedded = tokens + sin_cos_code(coords[:, 0:1], coords[:, 1:2])
    centred = embedded - jnp.mean(embedded, axis=-1, keepdims=True)
    rstd = lax.rsqrt(jnp.mean(centred * centred, axis=-1, keepdims=True) + EPSILON)
    xhat = centred * rstd
    normed = xhat.astype(BF)
    xhat_ref[...] = xhat
    rstd_ref[...] = jnp.broadcast_to(rstd, rstd_ref.shape)
    normed_ref[...] = normed
    packed = mm(normed, w_qkv_ref[...]).astype(BF)
    packed_ref[...] = packed
    live = (base + place_of(iota((ROWS, 1), 0))) < length
    out_grad = jnp.where(live, mm(order, cot_ref[0]), 0.0).astype(BF)
    grad_ref[...] = out_grad
    g = mm_nt(out_grad, w_out_ref[...]).astype(BF)
    g_ref[...] = g

    mask = head_mask(SLAB)
    key_col = place_of(iota((1, ROWS), 1))
    row = iota((GROUP * SLAB, 1), 0)
    query_col = RATE * (row % SLAB) + (row // SLAB) % RATE
    allowed = jnp.logical_or(base + key_col < length, key_col == query_col)
    scalars = []
    for group in range(2):
        q = jnp.where(mask, stack_slabs(packed[:, :D], group).astype(F32), 0.0).astype(BF)
        gs = stack_slabs(g, group).astype(F32)
        k = packed[:, D + group * WIDE : D + (group + 1) * WIDE]
        v = packed[:, 2 * D + group * WIDE : 2 * D + (group + 1) * WIDE]
        s = jnp.where(allowed, mm_nt(q, k) * SCALE, NEG_FILL)
        top = jnp.max(s, axis=-1, keepdims=True)
        e = jnp.exp(s - top)
        total = jnp.sum(e, axis=-1, keepdims=True)
        lse = top + jnp.log(total)
        out = mm((e / total).astype(BF), v)
        g_dot = jnp.sum(jnp.where(mask, gs * out, 0.0), axis=-1, keepdims=True)
        scalars.append((lse, g_dot))

    lane = iota((SLAB, BLOCK), 1)
    pad = jnp.zeros((SLAB, 128 - BLOCK), F32)
    for j in range(N_SEG):
        r0 = SLAB * ((2 * j) % RATE)
        columns = [[], []]
        for h in (2 * j, 2 * j + 1):
            at = (h % GROUP) * SLAB
            for which in range(2):
                columns[which] += list(split3(scalars[h // GROUP][which][at : at + SLAB]))
        for a in range(4):
            if a < 3:
                part = packed[r0 : r0 + 2 * SLAB, a * D + BLOCK * j : a * D + BLOCK * (j + 1)]
            else:
                part = g[r0 : r0 + 2 * SLAB, BLOCK * j : BLOCK * (j + 1)]
            part = part.astype(F32)
            part = jnp.where(lane < HEAD, part[:SLAB], part[SLAB:])
            part = jnp.concatenate([part, pad], axis=1)
            if a < 2:
                part = put_scalars(part, columns[a])
            message_ref[j, a] = part.astype(BF)

    core = lax.axis_index("core")
    zero = jnp.zeros((ROWS, 72), F32)
    wide = out_grad.astype(F32)
    for b in range(16):
        z_hi, xl, z_lo = b // 8, (b // 4) % 2, b % 4
        for c in range(2):
            dp = (z_hi * 4 + z_lo) * 4 + xl * 2 + c
            rel = (core + c) % 2
            block = jnp.concatenate([zero, wide[:, 24 * dp : 24 * dp + 24]], axis=1)
            blocks_ref[rel, :, BLOCK * b : BLOCK * (b + 1)] = block.astype(BF)


def dense_kernel(
    length_ref, packed_ref, g_ref, out_ref, back_ref, weight_ref, dweight_ref, sampled_out_ref
):
    length = length_ref[0]
    base = seg_index() * ROWS
    mask = head_mask(ROWS)
    small = head_mask(SLAB)
    row = iota((GROUP * ROWS, 1), 0)
    key_col = place_of(iota((1, ROWS), 1))
    query_col = place_of(row % ROWS)
    allowed = jnp.logical_or(base + key_col < length, key_col == query_col)
    free = (row % ROWS) // SLAB != (row // ROWS) % RATE

    def spread(part):
        return jnp.where(mask, jnp.concatenate([part.astype(F32)] * GROUP, axis=0), 0.0)

    def fold(stack):
        stack = jnp.where(mask, stack, 0.0)
        return sum(stack[ROWS * h : ROWS * (h + 1)] for h in range(GROUP))

    for group in range(2):
        lanes = slice(group * WIDE, (group + 1) * WIDE)
        q = spread(packed_ref[:, group * WIDE : (group + 1) * WIDE]).astype(BF)
        k = packed_ref[:, D + group * WIDE : D + (group + 1) * WIDE]
        v = packed_ref[:, 2 * D + group * WIDE : 2 * D + (group + 1) * WIDE]
        gm = spread(g_ref[:, lanes])
        gb = gm.astype(BF)
        s = jnp.where(allowed, mm_nt(q, k) * SCALE, NEG_FILL)
        e = jnp.exp(s - jnp.max(s, axis=-1, keepdims=True))
        p = e / jnp.sum(e, axis=-1, keepdims=True)
        out = mm(p.astype(BF), v)
        delta = jnp.sum(gm * out, axis=-1, keepdims=True)
        dp = mm_nt(gb, v)
        out_ref[:, lanes] = fold(out)
        free_p = jnp.where(free, p, 0.0)
        ds = (free_p * (dp - delta) * SCALE).astype(BF)
        back_ref[0, :, lanes] = fold(mm(ds, k))
        back_ref[1, :, lanes] = mm_tn(ds, q)
        back_ref[2, :, lanes] = mm_tn(free_p.astype(BF), gb)
        for h in range(GROUP):
            at = ROWS * h + SLAB * (h % RATE)
            to = slice(SLAB * h, SLAB * (h + 1))
            weight_ref[group, to] = p[at : at + SLAB]
            dweight_ref[group, to] = dp[at : at + SLAB]
            sampled_out_ref[group, to] = jnp.where(small[to], out[at : at + SLAB], 0.0)


def dilated_kernel(length_ref, message_ref, reply_ref):
    length = length_ref[0]
    j = seg_index()
    n = N_SEG * SLAB
    stack = []
    for a in range(4):
        stack.append(jnp.concatenate([message_ref[i, a] for i in range(N_SEG)], axis=0))
    q, k, v, g = stack
    lane = iota((n, 128), 1)
    scalar_lane = q.astype(F32), k.astype(F32)
    key = iota((1, n), 1)
    query = iota((n, 1), 0)
    outs = [jnp.zeros((n, 128), F32) for _ in range(4)]
    columns = [[], []]
    for half in range(2):
        mine = jnp.logical_and(lane >= HEAD * half, lane < HEAD * (half + 1))
        offset = (2 * j + half) % RATE

        def scalar(which):
            at = BLOCK + 3 * half
            x = scalar_lane[which]
            return x[:, at : at + 1] + x[:, at + 1 : at + 2] + x[:, at + 2 : at + 3]

        dense_lse, dense_dot = scalar(0), scalar(1)
        qm = jnp.where(mine, q.astype(F32), 0.0).astype(BF)
        gf = jnp.where(mine, g.astype(F32), 0.0)
        gm = gf.astype(BF)
        allowed = jnp.logical_or(RATE * key + offset < length, key == query)
        s = jnp.where(allowed, mm_nt(qm, k) * SCALE, NEG_FILL)
        top = jnp.max(s, axis=-1, keepdims=True)
        e = jnp.exp(s - top)
        total = jnp.sum(e, axis=-1, keepdims=True)
        lse = top + jnp.log(total)
        p = e / total
        out = mm(p.astype(BF), v)
        larger = jnp.maximum(lse, dense_lse)
        dense_part = jnp.exp(dense_lse - larger)
        own_part = jnp.exp(lse - larger)
        both = dense_part + own_part
        dense_part = dense_part / both
        own_part = own_part / both
        delta = dense_part * dense_dot + own_part * jnp.sum(gf * out, axis=-1, keepdims=True)
        p = p * own_part
        ds = (p * (mm_nt(gm, v) - delta) * SCALE).astype(BF)
        outs[0] = outs[0] + jnp.where(mine, mm(ds, k), 0.0)
        outs[1] = outs[1] + mm_tn(ds, qm)
        outs[2] = outs[2] + mm_tn(p.astype(BF), gm)
        outs[3] = outs[3] + jnp.where(mine, out * own_part, 0.0)
        columns[0] += list(split3(dense_part))
        columns[1] += list(split3(delta))
    outs[0] = put_scalars(outs[0], columns[0])
    outs[1] = put_scalars(outs[1], columns[1])
    for a in range(4):
        result = outs[a].astype(BF)
        for i in range(N_SEG):
            reply_ref[i, a] = result[SLAB * i : SLAB * (i + 1)]


def join_kernel(
    reply_ref, packed_ref, g_ref, out_ref, back_ref, weight_ref, dweight_ref, sampled_out_ref,
    blended_ref, packed_grad_ref, blocks_ref,
):
    small = head_mask(SLAB)
    shape = (ROWS, D)
    sampled = (iota(shape, 1) // HEAD) % RATE == iota(shape, 0) // SLAB

    def placed(a):
        row = jnp.concatenate(
            [reply_ref[j, a].astype(F32)[:, :BLOCK] for j in range(N_SEG)], axis=1
        )
        return jnp.where(sampled, jnp.concatenate([row] * RATE, axis=0), 0.0)

    def scalars(a, group):
        columns = []
        for h in range(GROUP * group, GROUP * (group + 1)):
            x = reply_ref[h // 2, a].astype(F32)
            at = BLOCK + 3 * (h % 2)
            columns.append(x[:, at : at + 1] + x[:, at + 1 : at + 2] + x[:, at + 2 : at + 3])
        return jnp.concatenate(columns, axis=0)

    parts = [[], [], [], []]
    for group in range(2):
        lanes = slice(group * WIDE, (group + 1) * WIDE)
        share, delta = scalars(0, group), scalars(1, group)
        q = jnp.where(small, stack_slabs(packed_ref[:, :D], group).astype(F32), 0.0).astype(BF)
        gm = jnp.where(small, stack_slabs(g_ref[...], group).astype(F32), 0.0).astype(BF)
        k = packed_ref[:, D + group * WIDE : D + (group + 1) * WIDE]
        p = weight_ref[group] * share
        ds = (p * (dweight_ref[group] - delta) * SCALE).astype(BF)
        parts[0].append(back_ref[0, :, lanes] + unstack_slabs(jnp.where(small, mm(ds, k), 0.0)))
        parts[1].append(back_ref[1, :, lanes] + mm_tn(ds, q))
        parts[2].append(back_ref[2, :, lanes] + mm_tn(p.astype(BF), gm))
        parts[3].append(unstack_slabs(sampled_out_ref[group] * share))
    whole = [jnp.concatenate(part, axis=1) for part in parts]
    blended_ref[...] = jnp.where(sampled, whole[3] + placed(3), out_ref[...]).astype(BF)
    grads = []
    for a in range(3):
        grad = (whole[a] + placed(a)).astype(BF)
        packed_grad_ref[:, a * D : (a + 1) * D] = grad
        grads.append(grad.astype(F32))
    grads = jnp.concatenate(grads, axis=1)
    core = lax.axis_index("core")
    zero = jnp.zeros((ROWS, 24), F32)
    for b in range(16):
        z_hi, xl, z_lo = b // 8, (b // 4) % 2, b % 4
        for c in range(2):
            dp = (z_hi * 4 + z_lo) * 4 + xl * 2 + c
            rel = (core + c) % 2
            block = jnp.concatenate([grads[:, 72 * dp : 72 * dp + 72], zero], axis=1)
            blocks_ref[rel, :, BLOCK * b : BLOCK * (b + 1)] = block.astype(BF)


def finish_kernel(
    length_ref, blended_ref, packed_grad_ref, xhat_ref, rstd_ref, w_qkv_ref, w_out_ref,
    layer_ref, token_grad_ref,
):
    length = length_ref[0]
    base = seg_index() * ROWS
    order = regroup()
    live = (base + place_of(iota((ROWS, 1), 0))) < length
    layer = jnp.where(live, mm(blended_ref[...], w_out_ref[...]), 0.0).astype(BF)
    layer_ref[0] = mm_tn(order, layer).astype(BF)
    dn = mm_nt(packed_grad_ref[...], w_qkv_ref[...])
    xhat = xhat_ref[...]
    mean = jnp.mean(dn, axis=-1, keepdims=True)
    slope = jnp.mean(dn * xhat, axis=-1, keepdims=True)
    dx = ((dn - mean - xhat * slope) * rstd_ref[:, 0:1]).astype(BF)
    token_grad_ref[0] = mm_tn(order, dx).astype(BF)


def weight_kernel(
    n0_ref, n1_ref, b0_ref, b1_ref, p0_ref, p1_ref, g0_ref, g1_ref, along_y_ref, along_x_ref
):
    xh, xl, y = lax.axis_index("xh"), lax.axis_index("xl"), lax.axis_index("y")
    left = jnp.concatenate([n0_ref[...], n1_ref[...], b0_ref[...], b1_ref[...]], axis=0)
    for part in range(4):
        z_hi, to_xl = part // 2, part % 2
        lanes = slice(part * WIDE, (part + 1) * WIDE)
        right = jnp.concatenate(
            [p0_ref[:, lanes], p1_ref[:, lanes], g0_ref[:, lanes], g1_ref[:, lanes]], axis=0
        )
        total = mm_tn(left, right).astype(BF)
        xl_rel = (to_xl + xl) % 2
        for s in range(N_SEG):
            xh_rel = (s // 4 + xh) % 2
            y_rel = (s % 4 - y + 4) % 4
            chunk = total[BLOCK * s : BLOCK * (s + 1)]
            if z_hi == 0:
                along_y_ref[y_rel, xh_rel, xl_rel] = chunk
            else:
                along_x_ref[xh_rel, xl_rel, y_rel] = chunk


def call(kernel, outs, specs, *args):
    return pl.pallas_call(
        kernel,
        out_shape=[jax.ShapeDtypeStruct(shape, dtype) for shape, dtype in outs],
        in_specs=specs,
        out_specs=[VMEM] * len(outs),
        compiler_params=pltpu.CompilerParams(vmem_limit_bytes=LIMIT),
    )(*args)


def to_core(x):
    return lax.ppermute(x, "core", [(0, 1), (1, 0)])


def along_y(x, k):
    return lax.ppermute(x, "y", [(i, (i + k) % 4) for i in range(4)])


def along_x(x, xh_rel, xl_rel):
    pairs = [(i, i ^ (2 * xl_rel + xh_rel)) for i in range(4)]
    return lax.ppermute(x, ("xl", "xh"), pairs)


def along_z(x, k):
    return lax.ppermute(x, "z", [(i, (i + k) % 8) for i in range(8)])


def add_up(parts):
    return sum(part.astype(F32) for part in parts)


def per_device(tokens, coords, lengths, w_qkv, w_out, cotangent):
    message, packed, g, xhat, rstd, normed, out_grad, grad_blocks = call(
        first_kernel,
        [
            ((N_SEG, 4, SLAB, 128), BF),
            ((ROWS, 3 * D), BF),
            ((ROWS, D), BF),
            ((ROWS, D), F32),
            ((ROWS, 128), F32),
            ((ROWS, D), BF),
            ((ROWS, D), BF),
            ((2, ROWS, 16 * BLOCK), BF),
        ],
        [SMEM] + [VMEM] * 5,
        lengths, tokens, coords, cotangent, w_qkv, w_out,
    )
    message = lax.all_to_all(message, ("xh", "y"), 0, 0, tiled=True)
    other_normed = to_core(normed)
    other_grad = to_core(grad_blocks[1])
    out, back, weight, dweight, sampled_out = call(
        dense_kernel,
        [
            ((ROWS, D), F32),
            ((3, ROWS, D), F32),
            ((2, GROUP * SLAB, ROWS), F32),
            ((2, GROUP * SLAB, ROWS), F32),
            ((2, GROUP * SLAB, WIDE), F32),
        ],
        [SMEM] + [VMEM] * 2,
        lengths, packed, g,
    )
    (reply,) = call(
        dilated_kernel, [((N_SEG, 4, SLAB, 128), BF)], [SMEM, VMEM], lengths, message
    )
    reply = lax.all_to_all(reply, ("xh", "y"), 0, 0, tiled=True)
    blended, packed_grad, blocks = call(
        join_kernel,
        [((ROWS, D), BF), ((ROWS, 3 * D), BF), ((2, ROWS, 16 * BLOCK), BF)],
        [VMEM] * 8,
        reply, packed, g, out, back, weight, dweight, sampled_out,
    )
    other_blended = to_core(blended)
    other_blocks = to_core(blocks[1])
    first, second = call(
        weight_kernel,
        [((4, 2, 2, BLOCK, WIDE), BF), ((2, 2, 4, BLOCK, WIDE), BF)],
        [VMEM] * 8,
        normed, other_normed, blended, other_blended,
        blocks[0], other_blocks, grad_blocks[0], other_grad,
    )
    layer_out, token_grad = call(
        finish_kernel,
        [((1, ROWS, D), BF), ((1, ROWS, D), BF)],
        [SMEM] + [VMEM] * 6,
        lengths, blended, packed_grad, xhat, rstd, w_qkv, w_out,
    )
    near = [(0, 1), (1, 0), (1, 1)]
    first = add_up([first[0]] + [along_y(first[k], k) for k in (1, 3, 2)]).astype(BF)
    second = add_up([second[0, 0]] + [along_x(second[a, b], a, b) for a, b in near]).astype(BF)
    first = add_up([first[0, 0]] + [along_x(first[a, b], a, b) for a, b in near]).astype(BF)
    second = add_up([second[0]] + [along_y(second[k], k) for k in (1, 3, 2)]).astype(BF)
    both = jnp.concatenate([first, second], axis=1)
    both = both.reshape(BLOCK, 8, BLOCK).transpose(1, 0, 2)
    z = lax.axis_index("z")
    both = jnp.roll(both, -z, axis=0)
    total = add_up([both[0]] + [along_z(both[k], k) for k in range(1, 8)])
    return layer_out, token_grad, total[:, :72], total[:, 72:]


def solution(mesh):
    devices = mesh.devices.reshape(8, 2, 2, 2, 4)
    fine = Mesh(devices, ("z", "xl", "core", "xh", "y"))
    dp, seg = ("z", "xl", "core"), ("xh", "y")
    placed = (P(dp, seg, None), P(dp, seg, None), P(dp), P(), P(), P(dp, seg, None))
    return jax.shard_map(
        per_device,
        mesh=fine,
        in_specs=placed,
        out_specs=(P(dp, seg, None), P(dp, seg, None), P(seg, dp), P(seg, dp)),
        check_vma=False,
    )
```

```python
import jax
import jax.numpy as jnp
from jax import lax
from jax.experimental import pallas as pl
from jax.experimental.pallas import tpu as pltpu
from jax.sharding import Mesh
from jax.sharding import PartitionSpec as P

HEADS = 16
RATE = 4
HEAD = 48
GROUP = 8
WIDE = GROUP * HEAD
ROWS = 128
SLAB = ROWS // RATE
D = 768
N_SEG = 8
BLOCK = 96
EPSILON = 1e-05
NEG_FILL = -1e30
SCALE = HEAD ** (-0.5)
BF = jnp.bfloat16
F32 = jnp.float32
VMEM = pl.BlockSpec(memory_space=pltpu.VMEM)
SMEM = pl.BlockSpec(memory_space=pltpu.SMEM)
ANY = pl.BlockSpec(memory_space=pl.ANY)
LIMIT = 20 * 1024 * 1024


def iota(shape, dim):
    return lax.broadcasted_iota(jnp.int32, shape, dim)


def mm(a, b):
    return lax.dot_general(a, b, (((1,), (0,)), ((), ())), preferred_element_type=F32)


def mm_nt(a, b):
    return lax.dot_general(a, b, (((1,), (1,)), ((), ())), preferred_element_type=F32)


def mm_tn(a, b):
    return lax.dot_general(a, b, (((0,), (0,)), ((), ())), preferred_element_type=F32)


def regroup():
    row, col = iota((ROWS, ROWS), 0), iota((ROWS, ROWS), 1)
    return (col == RATE * (row % SLAB) + row // SLAB).astype(BF)


def place_of(row):
    return RATE * (row % SLAB) + row // SLAB


def sin_cos_code(c0, c1):
    quarter = D // 4
    col = iota((1, D), 1)
    block = col // quarter
    freqs = jnp.exp((-jnp.log(F32(10000.0))) * (col - block * quarter).astype(F32) / quarter)
    angle = jnp.where(block < 2, c0, c1) * freqs
    turns = jnp.floor(angle * F32(0.6366197723675814) + F32(0.5))
    rest = angle - turns * F32(1.5703125)
    rest = rest - turns * F32(4.837512969970703e-4)
    rest = rest - turns * F32(7.549789948768648e-8)
    sq = rest * rest
    sine = rest + rest * sq * (
        F32(-1.6666654611e-1) + sq * (F32(8.3321608736e-3) + sq * F32(-1.9515295891e-4))
    )
    cosine = (
        F32(1.0)
        - F32(0.5) * sq
        + sq * sq * (F32(4.166664568298827e-2) + sq * (F32(-1.388731625493765e-3) + sq * F32(2.443315711809948e-5)))
    )
    quadrant = turns.astype(jnp.int32) + (block & 1)
    value = jnp.where((quadrant & 1) == 1, cosine, sine)
    return jnp.where((quadrant & 2) == 2, -value, value)


def head_mask(rows_per_head):
    shape = (GROUP * rows_per_head, WIDE)
    return iota(shape, 0) // rows_per_head == iota(shape, 1) // HEAD


def split3(x):
    hi = x.astype(BF)
    rest = x - hi.astype(F32)
    mid = rest.astype(BF)
    lo = (rest - mid.astype(F32)).astype(BF)
    return hi, mid, lo


def put_scalars(base, columns):
    lane = iota(base.shape, 1)
    for n, column in enumerate(columns):
        base = jnp.where(lane == BLOCK + n, column.astype(F32), base)
    return base


def stack_slabs(array, group):
    part = array[:, group * WIDE : (group + 1) * WIDE]
    return jnp.concatenate(
        [part[SLAB * (h % RATE) : SLAB * (h % RATE) + SLAB] for h in range(GROUP)], axis=0
    )


def unstack_slabs(stack):
    return jnp.concatenate(
        [
            stack[SLAB * o : SLAB * o + SLAB] + stack[SLAB * (o + RATE) : SLAB * (o + RATE) + SLAB]
            for o in range(RATE)
        ],
        axis=0,
    )


def seg_index():
    return lax.axis_index("xh") * 4 + lax.axis_index("y")


def first_kernel(
    length_ref, coord_ref, tok_ref, w_qkv_ref, cot_ref, w_out_ref,
    message_ref, packed_ref, g_ref, xhat_ref, rstd_ref, normed_ref, blocks_ref,
):
    length = length_ref[0]
    base = seg_index() * ROWS
    order = regroup()
    coords = mm_nt(order, coord_ref[0].astype(F32).astype(BF))
    code = sin_cos_code(coords[:, 0:1], coords[:, 1:2])
    tokens = mm(order, tok_ref[0])
    embedded = tokens + code
    centred = embedded - jnp.mean(embedded, axis=-1, keepdims=True)
    rstd = lax.rsqrt(jnp.mean(centred * centred, axis=-1, keepdims=True) + EPSILON)
    xhat = centred * rstd
    normed = xhat.astype(BF)
    xhat_ref[...] = xhat
    rstd_ref[...] = jnp.broadcast_to(rstd, rstd_ref.shape)
    normed_ref[...] = normed
    packed = mm(normed, w_qkv_ref[...]).astype(BF)
    packed_ref[...] = packed
    live = (base + place_of(iota((ROWS, 1), 0))) < length
    out_grad = jnp.where(live, mm(order, cot_ref[0]), 0.0).astype(BF)
    g = mm_nt(out_grad, w_out_ref[...]).astype(BF)
    g_ref[...] = g

    mask = head_mask(SLAB)
    key_col = place_of(iota((1, ROWS), 1))
    row = iota((GROUP * SLAB, 1), 0)
    query_col = RATE * (row % SLAB) + (row // SLAB) % RATE
    allowed = jnp.logical_or(base + key_col < length, key_col == query_col)
    scalars = []
    for group in range(2):
        q = jnp.where(mask, stack_slabs(packed[:, :D], group).astype(F32), 0.0).astype(BF)
        gs = stack_slabs(g, group).astype(F32)
        k = packed[:, D + group * WIDE : D + (group + 1) * WIDE]
        v = packed[:, 2 * D + group * WIDE : 2 * D + (group + 1) * WIDE]
        s = jnp.where(allowed, mm_nt(q, k) * SCALE, NEG_FILL)
        top = jnp.max(s, axis=-1, keepdims=True)
        e = jnp.exp(s - top)
        total = jnp.sum(e, axis=-1, keepdims=True)
        lse = top + jnp.log(total)
        out = mm((e / total).astype(BF), v)
        g_dot = jnp.sum(jnp.where(mask, gs * out, 0.0), axis=-1, keepdims=True)
        scalars.append((lse, g_dot))

    lane = iota((SLAB, BLOCK), 1)
    pad = jnp.zeros((SLAB, 128 - BLOCK), F32)
    for j in range(N_SEG):
        r0 = SLAB * ((2 * j) % RATE)
        columns = [[], []]
        for h in (2 * j, 2 * j + 1):
            at = (h % GROUP) * SLAB
            for which in range(2):
                columns[which] += list(split3(scalars[h // GROUP][which][at : at + SLAB]))
        for a in range(4):
            if a < 3:
                part = packed[r0 : r0 + 2 * SLAB, a * D + BLOCK * j : a * D + BLOCK * (j + 1)]
            else:
                part = g[r0 : r0 + 2 * SLAB, BLOCK * j : BLOCK * (j + 1)]
            part = part.astype(F32)
            part = jnp.where(lane < HEAD, part[:SLAB], part[SLAB:])
            part = jnp.concatenate([part, pad], axis=1)
            if a < 2:
                part = put_scalars(part, columns[a])
            message_ref[j, a] = part.astype(BF)

    core = lax.axis_index("core")
    zero = jnp.zeros((ROWS, 72), F32)
    wide = out_grad.astype(F32)
    for b in range(16):
        xl, z = b // 8, b % 8
        for c in range(2):
            dp = z * 4 + xl * 2 + c
            rel = (core + c) % 2
            block = jnp.concatenate([zero, wide[:, 24 * dp : 24 * dp + 24]], axis=1)
            blocks_ref[rel, :, BLOCK * b : BLOCK * (b + 1)] = block.astype(BF)


def dense_kernel(
    length_ref, packed_ref, g_ref, out_ref, back_ref, weight_ref, dweight_ref
):
    length = length_ref[0]
    base = seg_index() * ROWS
    mask = head_mask(ROWS)
    row = iota((GROUP * ROWS, 1), 0)
    key_col = place_of(iota((1, ROWS), 1))
    query_col = place_of(row % ROWS)
    allowed = jnp.logical_or(base + key_col < length, key_col == query_col)
    free = (row % ROWS) // SLAB != (row // ROWS) % RATE

    def spread(part):
        return jnp.where(mask, jnp.concatenate([part.astype(F32)] * GROUP, axis=0), 0.0)

    def fold(stack):
        stack = jnp.where(mask, stack, 0.0)
        return sum(stack[ROWS * h : ROWS * (h + 1)] for h in range(GROUP))

    for group in range(2):
        lanes = slice(group * WIDE, (group + 1) * WIDE)
        q = spread(packed_ref[:, group * WIDE : (group + 1) * WIDE]).astype(BF)
        k = packed_ref[:, D + group * WIDE : D + (group + 1) * WIDE]
        v = packed_ref[:, 2 * D + group * WIDE : 2 * D + (group + 1) * WIDE]
        gm = spread(g_ref[:, lanes])
        gb = gm.astype(BF)
        s = jnp.where(allowed, mm_nt(q, k) * SCALE, NEG_FILL)
        e = jnp.exp(s - jnp.max(s, axis=-1, keepdims=True))
        p = e / jnp.sum(e, axis=-1, keepdims=True)
        out = mm(p.astype(BF), v)
        delta = jnp.sum(gm * out, axis=-1, keepdims=True)
        dp = mm_nt(gb, v)
        out_ref[:, lanes] = fold(out)
        free_p = jnp.where(free, p, 0.0)
        ds = (free_p * (dp - delta) * SCALE).astype(BF)
        back_ref[0, :, lanes] = fold(mm(ds, k))
        back_ref[1, :, lanes] = mm_tn(ds, q)
        back_ref[2, :, lanes] = mm_tn(free_p.astype(BF), gb)
        for h in range(GROUP):
            at = ROWS * h + SLAB * (h % RATE)
            to = slice(SLAB * h, SLAB * (h + 1))
            weight_ref[group, to] = p[at : at + SLAB]
            dweight_ref[group, to] = dp[at : at + SLAB]


def dilated_kernel(length_ref, message_ref, reply_ref):
    length = length_ref[0]
    j = seg_index()
    n = N_SEG * SLAB
    stack = []
    for a in range(4):
        stack.append(jnp.concatenate([message_ref[i, a] for i in range(N_SEG)], axis=0))
    q, k, v, g = stack
    lane = iota((n, 128), 1)
    scalar_lane = q.astype(F32), k.astype(F32)
    key = iota((1, n), 1)
    query = iota((n, 1), 0)
    outs = [jnp.zeros((n, 128), F32) for _ in range(4)]
    columns = [[], []]
    for half in range(2):
        mine = jnp.logical_and(lane >= HEAD * half, lane < HEAD * (half + 1))
        offset = (2 * j + half) % RATE

        def scalar(which):
            at = BLOCK + 3 * half
            x = scalar_lane[which]
            return x[:, at : at + 1] + x[:, at + 1 : at + 2] + x[:, at + 2 : at + 3]

        dense_lse, dense_dot = scalar(0), scalar(1)
        qm = jnp.where(mine, q.astype(F32), 0.0).astype(BF)
        gf = jnp.where(mine, g.astype(F32), 0.0)
        gm = gf.astype(BF)
        allowed = jnp.logical_or(RATE * key + offset < length, key == query)
        s = jnp.where(allowed, mm_nt(qm, k) * SCALE, NEG_FILL)
        top = jnp.max(s, axis=-1, keepdims=True)
        e = jnp.exp(s - top)
        total = jnp.sum(e, axis=-1, keepdims=True)
        lse = top + jnp.log(total)
        p = e / total
        out = mm(p.astype(BF), v)
        larger = jnp.maximum(lse, dense_lse)
        dense_part = jnp.exp(dense_lse - larger)
        own_part = jnp.exp(lse - larger)
        both = dense_part + own_part
        dense_part = dense_part / both
        own_part = own_part / both
        delta = dense_part * dense_dot + own_part * jnp.sum(gf * out, axis=-1, keepdims=True)
        p = p * own_part
        ds = (p * (mm_nt(gm, v) - delta) * SCALE).astype(BF)
        outs[0] = outs[0] + jnp.where(mine, mm(ds, k), 0.0)
        outs[1] = outs[1] + mm_tn(ds, qm)
        outs[2] = outs[2] + mm_tn(p.astype(BF), gm)
        outs[3] = outs[3] + jnp.where(mine, out * own_part, 0.0)
        columns[0] += list(split3(dense_part))
        columns[1] += list(split3(delta))
    outs[0] = put_scalars(outs[0], columns[0])
    outs[1] = put_scalars(outs[1], columns[1])
    for a in range(4):
        result = outs[a].astype(BF)
        for i in range(N_SEG):
            reply_ref[i, a] = result[SLAB * i : SLAB * (i + 1)]


def join_kernel(
    reply_ref, packed_ref, g_ref, weight_ref, dweight_ref, back_ref, out_ref,
    blended_ref, packed_grad_ref, blocks_ref,
):
    small = head_mask(SLAB)
    shape = (ROWS, D)
    sampled = (iota(shape, 1) // HEAD) % RATE == iota(shape, 0) // SLAB

    def placed(a):
        row = jnp.concatenate(
            [reply_ref[j, a].astype(F32)[:, :BLOCK] for j in range(N_SEG)], axis=1
        )
        return jnp.where(sampled, jnp.concatenate([row] * RATE, axis=0), 0.0)

    def scalars(a, group):
        columns = []
        for h in range(GROUP * group, GROUP * (group + 1)):
            x = reply_ref[h // 2, a].astype(F32)
            at = BLOCK + 3 * (h % 2)
            columns.append(x[:, at : at + 1] + x[:, at + 1 : at + 2] + x[:, at + 2 : at + 3])
        return jnp.concatenate(columns, axis=0)

    parts = [[], [], [], []]
    for group in range(2):
        lanes = slice(group * WIDE, (group + 1) * WIDE)
        share, delta = scalars(0, group), scalars(1, group)
        q = jnp.where(small, stack_slabs(packed_ref[:, :D], group).astype(F32), 0.0).astype(BF)
        gm = jnp.where(small, stack_slabs(g_ref[...], group).astype(F32), 0.0).astype(BF)
        k = packed_ref[:, D + group * WIDE : D + (group + 1) * WIDE]
        p = weight_ref[group] * share
        ds = (p * (dweight_ref[group] - delta) * SCALE).astype(BF)
        parts[0].append(back_ref[0, :, lanes] + unstack_slabs(jnp.where(small, mm(ds, k), 0.0)))
        parts[1].append(back_ref[1, :, lanes] + mm_tn(ds, q))
        parts[2].append(back_ref[2, :, lanes] + mm_tn(p.astype(BF), gm))
        parts[3].append(unstack_slabs(jnp.where(small, share, 0.0)))
    whole = [jnp.concatenate(part, axis=1) for part in parts]
    out = out_ref[...]
    blended_ref[...] = jnp.where(sampled, whole[3] * out + placed(3), out).astype(BF)
    grads = []
    for a in range(3):
        grad = (whole[a] + placed(a)).astype(BF)
        packed_grad_ref[:, a * D : (a + 1) * D] = grad
        grads.append(grad.astype(F32))
    grads = jnp.concatenate(grads, axis=1)
    core = lax.axis_index("core")
    zero = jnp.zeros((ROWS, 24), F32)
    for b in range(16):
        xl, z = b // 8, b % 8
        for c in range(2):
            dp = z * 4 + xl * 2 + c
            rel = (core + c) % 2
            block = jnp.concatenate([grads[:, 72 * dp : 72 * dp + 72], zero], axis=1)
            blocks_ref[rel, :, BLOCK * b : BLOCK * (b + 1)] = block.astype(BF)


def finish_kernel(
    length_ref, blended_ref, w_out_ref, packed_grad_ref, w_qkv_ref, xhat_ref, rstd_ref,
    layer_ref, token_grad_ref, done_ref,
):
    length = length_ref[0]
    base = seg_index() * ROWS
    order = regroup()
    live = (base + place_of(iota((ROWS, 1), 0))) < length
    layer = jnp.where(live, mm(blended_ref[...], w_out_ref[...]), 0.0).astype(BF)
    layer_ref[0] = mm_tn(order, layer).astype(BF)
    dn = mm_nt(packed_grad_ref[...], w_qkv_ref[...])
    xhat = xhat_ref[...]
    mean = jnp.mean(dn, axis=-1, keepdims=True)
    slope = jnp.mean(dn * xhat, axis=-1, keepdims=True)
    dx = ((dn - mean - xhat * slope) * rstd_ref[:, 0:1]).astype(BF)
    token_grad_ref[0] = mm_tn(order, dx).astype(BF)
    done_ref[...] = jnp.zeros(done_ref.shape, F32)


def weight_kernel(n0_ref, n1_ref, b0_ref, b1_ref, p0_ref, p1_ref, g0_ref, g1_ref, out_ref):
    xh, xl, y = lax.axis_index("xh"), lax.axis_index("xl"), lax.axis_index("y")
    core = lax.axis_index("core")
    left = jnp.concatenate([n0_ref[...], n1_ref[...], b0_ref[...], b1_ref[...]], axis=0)
    for part in range(4):
        to_xl, half = part // 2, part % 2
        lanes = slice(part * WIDE, (part + 1) * WIDE)
        right = jnp.concatenate(
            [p0_ref[:, lanes], p1_ref[:, lanes], g0_ref[:, lanes], g1_ref[:, lanes]], axis=0
        )
        total = mm_tn(left, right).astype(BF)
        for s in range(N_SEG):
            x_rel = 2 * ((to_xl + xl) % 2) + (s // 4 + xh) % 2
            y_rel = (s % 4 - y + 4) % 4
            first = jnp.where(core == 0, y_rel, x_rel)
            second = jnp.where(core == 0, x_rel, y_rel)
            out_ref[first, second, :, half * WIDE : (half + 1) * WIDE] = total[
                BLOCK * s : BLOCK * (s + 1)
            ]


def first_sum_kernel(own_ref, a_ref, b_ref, c_ref, out_ref):
    for k in range(4):
        total = own_ref[0, k].astype(F32) + a_ref[k].astype(F32)
        total = total + (b_ref[k].astype(F32) + c_ref[k].astype(F32))
        out_ref[k] = total.astype(BF)


def second_sum_kernel(own_ref, a_ref, b_ref, c_ref, out_ref):
    total = own_ref[0].astype(F32) + a_ref[...].astype(F32)
    total = total + (b_ref[...].astype(F32) + c_ref[...].astype(F32))
    for z in range(8):
        out_ref[z] = total[:, BLOCK * z : BLOCK * (z + 1)].astype(BF)


def last_sum_kernel(parts_ref, in_ref, out_ref):
    total = parts_ref[0].astype(F32)
    for z in range(1, 8):
        total = total + parts_ref[z].astype(F32)
    total = total.T
    in_ref[...] = total[:72]
    out_ref[...] = total[72:]


class Held:
    def __init__(self, source, target, sem):
        self.target = target
        self.copy = pltpu.make_async_copy(source, target, sem)
        self.copy.start()
        self.here = False

    def __getitem__(self, index):
        if not self.here:
            self.copy.wait()
            self.here = True
        return self.target[index]


def call(kernel, outs, *inputs):
    specs = {"s": SMEM, "v": VMEM, "f": ANY, "h": ANY, "n": ANY}
    kinds = [kind for kind, _ in inputs]
    arrays = [
        pltpu.with_memory_space_constraint(x, pltpu.HBM) if kind == "h" else x
        for kind, x in inputs
    ]
    fetched = [x for kind, x in inputs if kind in "fh"]

    def body(*refs):
        n, m = len(kinds), len(outs)
        slots = list(refs[n + m : -1]) if fetched else []
        given = []
        for kind, ref in zip(kinds, refs[:n]):
            if kind in "fh":
                given.append(Held(ref, slots.pop(0), refs[-1].at[len(slots)]))
            elif kind != "n":
                given.append(ref)
        kernel(*given, *refs[n : n + m])

    scratch = [pltpu.VMEM(x.shape, x.dtype) for x in fetched]
    if fetched:
        scratch.append(pltpu.SemaphoreType.DMA((len(fetched),)))
    return pl.pallas_call(
        body,
        out_shape=[jax.ShapeDtypeStruct(shape, dtype) for shape, dtype in outs],
        in_specs=[specs[kind] for kind in kinds],
        out_specs=[VMEM] * len(outs),
        scratch_shapes=scratch,
        compiler_params=pltpu.CompilerParams(vmem_limit_bytes=LIMIT),
        name=kernel.__name__,
    )(*arrays)


def to_core(x):
    return lax.ppermute(x, "core", [(0, 1), (1, 0)])


def swap(x, k, stage):
    pairs = []
    for i in range(32):
        xl, core, xh, y = i // 16, (i // 8) % 2, (i // 4) % 2, i % 4
        if core == stage:
            y = (y + k) % 4
        else:
            xl, xh = xl ^ (k // 2), xh ^ (k % 2)
        pairs.append((i, ((xl * 2 + core) * 2 + xh) * 4 + y))
    return lax.ppermute(x, ("xl", "core", "xh", "y"), pairs)


def per_device(tokens, coords, lengths, w_qkv, w_out, cotangent):
    message, packed, g, xhat, rstd, normed, grad_blocks = call(
        first_kernel,
        [
            ((N_SEG, 4, SLAB, 128), BF),
            ((ROWS, 3 * D), BF),
            ((ROWS, D), BF),
            ((ROWS, D), F32),
            ((ROWS, 128), F32),
            ((ROWS, D), BF),
            ((2, ROWS, 16 * BLOCK), BF),
        ],
        ("s", lengths),
        ("h", jnp.transpose(coords, (0, 2, 1))),
        ("h", tokens),
        ("h", w_qkv),
        ("h", cotangent),
        ("h", w_out),
    )
    message = lax.all_to_all(message, ("xh", "y"), 0, 0, tiled=True)
    other_normed = to_core(normed)
    other_grad = to_core(grad_blocks[1])
    out, back, weight, dweight = call(
        dense_kernel,
        [
            ((ROWS, D), F32),
            ((3, ROWS, D), F32),
            ((2, GROUP * SLAB, ROWS), F32),
            ((2, GROUP * SLAB, ROWS), F32),
        ],
        ("s", lengths),
        ("v", packed),
        ("v", g),
    )
    (reply,) = call(
        dilated_kernel,
        [((N_SEG, 4, SLAB, 128), BF)],
        ("s", lengths),
        ("v", message),
        ("n", dweight),
        ("n", other_normed),
        ("n", other_grad),
    )
    reply = lax.all_to_all(reply, ("xh", "y"), 0, 0, tiled=True)
    blended, packed_grad, blocks = call(
        join_kernel,
        [((ROWS, D), BF), ((ROWS, 3 * D), BF), ((2, ROWS, 16 * BLOCK), BF)],
        ("v", reply),
        ("v", packed),
        ("v", g),
        ("h", weight),
        ("v", dweight),
        ("v", back),
        ("h", out),
    )
    other_blended = to_core(blended)
    other_blocks = to_core(blocks[1])
    (partial,) = call(
        weight_kernel,
        [((4, 4, BLOCK, D), BF)],
        ("f", normed),
        ("f", other_normed),
        ("v", blended),
        ("v", other_blended),
        ("v", blocks[0]),
        ("v", other_blocks),
        ("f", grad_blocks[0]),
        ("f", other_grad),
    )
    layer_out, token_grad, done = call(
        finish_kernel,
        [((1, ROWS, D), BF), ((1, ROWS, D), BF), ((8, 128), F32)],
        ("s", lengths),
        ("f", blended),
        ("h", w_out),
        ("f", packed_grad),
        ("h", w_qkv),
        ("h", xhat),
        ("h", rstd),
    )
    arrived = [swap(partial[k], k, 0) for k in (1, 2, 3)]
    (partial,) = call(
        first_sum_kernel,
        [((4, BLOCK, D), BF)],
        ("v", partial),
        *[("v", x) for x in arrived],
        ("n", done),
    )
    arrived = [swap(partial[k], k, 1) for k in (1, 2, 3)]
    (partial,) = call(
        second_sum_kernel,
        [((8, BLOCK, BLOCK), BF)],
        ("v", partial),
        *[("v", x) for x in arrived],
    )
    arrived = lax.all_to_all(partial, "z", 0, 0, tiled=True)
    grad_in, grad_out = call(
        last_sum_kernel, [((72, BLOCK), F32), ((24, BLOCK), F32)], ("v", arrived)
    )
    return layer_out, token_grad, grad_in.T, grad_out.T


def solution(mesh):
    devices = mesh.devices.reshape(8, 2, 2, 2, 4)
    fine = Mesh(devices, ("z", "xl", "core", "xh", "y"))
    dp, seg = ("z", "xl", "core"), ("xh", "y")
    placed = (P(dp, seg, None), P(dp, seg, None), P(dp), P(), P(), P(dp, seg, None))
    return jax.shard_map(
        per_device,
        mesh=fine,
        in_specs=placed,
        out_specs=(P(dp, seg, None), P(dp, seg, None), P(seg, dp), P(seg, dp)),
        check_vma=False,
    )
```

```python
import jax
import jax.numpy as jnp
from jax import lax
from jax.experimental import pallas as pl
from jax.experimental.pallas import tpu as pltpu
from jax.sharding import Mesh
from jax.sharding import PartitionSpec as P

HEADS = 16
RATE = 4
HEAD = 48
GROUP = 8
WIDE = GROUP * HEAD
ROWS = 128
SLAB = ROWS // RATE
D = 768
N_SEG = 8
BLOCK = 96
QKV_HALF = 640
OUT_HALF = 256
EPSILON = 1e-05
NEG_FILL = -1e30
SCALE = HEAD ** (-0.5)
BF = jnp.bfloat16
F32 = jnp.float32
VMEM = pl.BlockSpec(memory_space=pltpu.VMEM)
SMEM = pl.BlockSpec(memory_space=pltpu.SMEM)
ANY = pl.BlockSpec(memory_space=pl.ANY)
LIMIT = 20 * 1024 * 1024


def iota(shape, dim):
    return lax.broadcasted_iota(jnp.int32, shape, dim)


def mm(a, b):
    return lax.dot_general(a, b, (((1,), (0,)), ((), ())), preferred_element_type=F32)


def mm_nt(a, b):
    return lax.dot_general(a, b, (((1,), (1,)), ((), ())), preferred_element_type=F32)


def mm_tn(a, b):
    return lax.dot_general(a, b, (((0,), (0,)), ((), ())), preferred_element_type=F32)


def regroup():
    row, col = iota((ROWS, ROWS), 0), iota((ROWS, ROWS), 1)
    return (col == RATE * (row % SLAB) + row // SLAB).astype(BF)


def place_of(row):
    return RATE * (row % SLAB) + row // SLAB


def sin_cos_code(c0, c1):
    quarter = D // 4
    col = iota((1, D), 1)
    block = col // quarter
    freqs = jnp.exp((-jnp.log(F32(10000.0))) * (col - block * quarter).astype(F32) / quarter)
    angle = jnp.where(block < 2, c0, c1) * freqs
    turns = jnp.floor(angle * F32(0.6366197723675814) + F32(0.5))
    rest = angle - turns * F32(1.5703125)
    rest = rest - turns * F32(4.837512969970703e-4)
    rest = rest - turns * F32(7.549789948768648e-8)
    sq = rest * rest
    sine = rest + rest * sq * (
        F32(-1.6666654611e-1) + sq * (F32(8.3321608736e-3) + sq * F32(-1.9515295891e-4))
    )
    cosine = (
        F32(1.0)
        - F32(0.5) * sq
        + sq * sq * (F32(4.166664568298827e-2) + sq * (F32(-1.388731625493765e-3) + sq * F32(2.443315711809948e-5)))
    )
    quadrant = turns.astype(jnp.int32) + (block & 1)
    value = jnp.where((quadrant & 1) == 1, cosine, sine)
    return jnp.where((quadrant & 2) == 2, -value, value)


def head_mask(rows_per_head):
    shape = (GROUP * rows_per_head, WIDE)
    return iota(shape, 0) // rows_per_head == iota(shape, 1) // HEAD


def split3(x):
    hi = x.astype(BF)
    rest = x - hi.astype(F32)
    mid = rest.astype(BF)
    lo = (rest - mid.astype(F32)).astype(BF)
    return hi, mid, lo


def put_scalars(base, columns):
    lane = iota(base.shape, 1)
    for n, column in enumerate(columns):
        base = jnp.where(lane == BLOCK + n, column.astype(F32), base)
    return base


def stack_slabs(array, group):
    part = array[:, group * WIDE : (group + 1) * WIDE]
    return jnp.concatenate(
        [part[SLAB * (h % RATE) : SLAB * (h % RATE) + SLAB] for h in range(GROUP)], axis=0
    )


def unstack_slabs(stack):
    return jnp.concatenate(
        [
            stack[SLAB * o : SLAB * o + SLAB] + stack[SLAB * (o + RATE) : SLAB * (o + RATE) + SLAB]
            for o in range(RATE)
        ],
        axis=0,
    )


def seg_index():
    return lax.axis_index("xh") * 4 + lax.axis_index("y")


def first_kernel(
    length_ref, coord_ref, cot_ref, tok_ref, w_out_ref, w_qkv_ref,
    message_ref, packed_ref, g_ref, xhat_out, out_grad_out,
):
    length = length_ref[0]
    base = seg_index() * ROWS
    order = regroup()
    coords = coord_ref[0].astype(F32).astype(BF)
    cotangent, tokens, w_out = cot_ref[0], tok_ref[0], w_out_ref[...]
    live = (base + place_of(iota((ROWS, 1), 0))) < length
    out_grad = jnp.where(live, mm(order, cotangent), 0.0).astype(BF)
    out_grad_out.put(out_grad)
    g = mm_nt(out_grad, w_out).astype(BF)
    g_ref[...] = g
    coords = mm_nt(order, coords)
    embedded = mm(order, tokens) + sin_cos_code(coords[:, 0:1], coords[:, 1:2])
    centred = embedded - jnp.mean(embedded, axis=-1, keepdims=True)
    rstd = lax.rsqrt(jnp.mean(centred * centred, axis=-1, keepdims=True) + EPSILON)
    xhat = centred * rstd
    xhat_out.put(jnp.concatenate([xhat, jnp.broadcast_to(rstd, (ROWS, 128))], axis=1))
    packed = mm(xhat.astype(BF), w_qkv_ref[...]).astype(BF)
    packed_ref[...] = packed

    mask = head_mask(SLAB)
    key_col = place_of(iota((1, ROWS), 1))
    row = iota((GROUP * SLAB, 1), 0)
    query_col = RATE * (row % SLAB) + (row // SLAB) % RATE
    allowed = jnp.logical_or(base + key_col < length, key_col == query_col)
    scalars = []
    for group in range(2):
        q = jnp.where(mask, stack_slabs(packed[:, :D], group).astype(F32), 0.0).astype(BF)
        gs = stack_slabs(g, group).astype(F32)
        k = packed[:, D + group * WIDE : D + (group + 1) * WIDE]
        v = packed[:, 2 * D + group * WIDE : 2 * D + (group + 1) * WIDE]
        s = jnp.where(allowed, mm_nt(q, k) * SCALE, NEG_FILL)
        top = jnp.max(s, axis=-1, keepdims=True)
        e = jnp.exp(s - top)
        total = jnp.sum(e, axis=-1, keepdims=True)
        lse = top + jnp.log(total)
        out = mm((e / total).astype(BF), v)
        g_dot = jnp.sum(jnp.where(mask, gs * out, 0.0), axis=-1, keepdims=True)
        scalars.append((lse, g_dot))

    lane = iota((SLAB, BLOCK), 1)
    pad = jnp.zeros((SLAB, 128 - BLOCK), F32)
    for j in range(N_SEG):
        r0 = SLAB * ((2 * j) % RATE)
        columns = [[], []]
        for h in (2 * j, 2 * j + 1):
            at = (h % GROUP) * SLAB
            for which in range(2):
                columns[which] += list(split3(scalars[h // GROUP][which][at : at + SLAB]))
        for a in range(4):
            if a < 3:
                part = packed[r0 : r0 + 2 * SLAB, a * D + BLOCK * j : a * D + BLOCK * (j + 1)]
            else:
                part = g[r0 : r0 + 2 * SLAB, BLOCK * j : BLOCK * (j + 1)]
            part = part.astype(F32)
            part = jnp.where(lane < HEAD, part[:SLAB], part[SLAB:])
            part = jnp.concatenate([part, pad], axis=1)
            if a < 2:
                part = put_scalars(part, columns[a])
            message_ref[j, a] = part.astype(BF)


def by_owner(array, width, padded):
    pad = jnp.zeros((ROWS, padded - 8 * width), array.dtype)
    sides = []
    for c in range(2):
        pieces = []
        for z_hi in range(2):
            for xl in range(2):
                for z_lo in range(4):
                    dp = (z_hi * 4 + z_lo) * 4 + xl * 2 + c
                    pieces.append(array[:, width * dp : width * (dp + 1)])
            pieces.append(pad)
        sides.append(jnp.concatenate(pieces, axis=1).astype(BF))
    first = lax.axis_index("core") == 0
    return jnp.where(first, sides[0], sides[1]), jnp.where(first, sides[1], sides[0])


def dense_kernel(
    length_ref, packed_ref, g_ref, xhat_ref, out_grad_ref,
    back_ref, soft_ref, early_ref,
):
    length = length_ref[0]
    base = seg_index() * ROWS
    mask = head_mask(ROWS)
    row = iota((GROUP * ROWS, 1), 0)
    key_col = place_of(iota((1, ROWS), 1))
    query_col = place_of(row % ROWS)
    allowed = jnp.logical_or(base + key_col < length, key_col == query_col)
    free = (row % ROWS) // SLAB != (row // ROWS) % RATE

    def spread(part):
        return jnp.where(mask, jnp.concatenate([part.astype(F32)] * GROUP, axis=0), 0.0)

    def fold(stack):
        stack = jnp.where(mask, stack, 0.0)
        return sum(stack[ROWS * h : ROWS * (h + 1)] for h in range(GROUP))

    for group in range(2):
        lanes = slice(group * WIDE, (group + 1) * WIDE)
        q = spread(packed_ref[:, group * WIDE : (group + 1) * WIDE]).astype(BF)
        k = packed_ref[:, D + group * WIDE : D + (group + 1) * WIDE]
        v = packed_ref[:, 2 * D + group * WIDE : 2 * D + (group + 1) * WIDE]
        gm = spread(g_ref[:, lanes])
        gb = gm.astype(BF)
        s = jnp.where(allowed, mm_nt(q, k) * SCALE, NEG_FILL)
        e = jnp.exp(s - jnp.max(s, axis=-1, keepdims=True))
        p = e / jnp.sum(e, axis=-1, keepdims=True)
        out = mm(p.astype(BF), v)
        delta = jnp.sum(gm * out, axis=-1, keepdims=True)
        dp = mm_nt(gb, v)
        back_ref[3, :, lanes] = fold(out)
        free_p = jnp.where(free, p, 0.0)
        ds = (free_p * (dp - delta) * SCALE).astype(BF)
        back_ref[0, :, lanes] = fold(mm(ds, k))
        back_ref[1, :, lanes] = mm_tn(ds, q)
        back_ref[2, :, lanes] = mm_tn(free_p.astype(BF), gb)
        for h in range(GROUP):
            at = ROWS * h + SLAB * (h % RATE)
            to = slice(SLAB * h, SLAB * (h + 1))
            soft_ref[group, 0, to] = p[at : at + SLAB]
            soft_ref[group, 1, to] = dp[at : at + SLAB]
    mine, theirs = by_owner(out_grad_ref[...].astype(F32), 24, OUT_HALF)
    early_ref[:, : 2 * OUT_HALF] = theirs
    early_ref[:, 2 * OUT_HALF : 4 * OUT_HALF] = mine
    early_ref[:, 4 * OUT_HALF :] = xhat_ref[:, :D].astype(BF)


def dilated_kernel(length_ref, message_ref, reply_ref):
    length = length_ref[0]
    j = seg_index()
    n = N_SEG * SLAB
    stack = []
    for a in range(4):
        stack.append(jnp.concatenate([message_ref[i, a] for i in range(N_SEG)], axis=0))
    q, k, v, g = stack
    lane = iota((n, 128), 1)
    scalar_lane = q.astype(F32), k.astype(F32)
    key = iota((1, n), 1)
    query = iota((n, 1), 0)
    outs = [jnp.zeros((n, 128), F32) for _ in range(4)]
    columns = [[], []]
    for half in range(2):
        mine = jnp.logical_and(lane >= HEAD * half, lane < HEAD * (half + 1))
        offset = (2 * j + half) % RATE

        def scalar(which):
            at = BLOCK + 3 * half
            x = scalar_lane[which]
            return x[:, at : at + 1] + x[:, at + 1 : at + 2] + x[:, at + 2 : at + 3]

        dense_lse, dense_dot = scalar(0), scalar(1)
        qm = jnp.where(mine, q.astype(F32), 0.0).astype(BF)
        gf = jnp.where(mine, g.astype(F32), 0.0)
        gm = gf.astype(BF)
        allowed = jnp.logical_or(RATE * key + offset < length, key == query)
        s = jnp.where(allowed, mm_nt(qm, k) * SCALE, NEG_FILL)
        top = jnp.max(s, axis=-1, keepdims=True)
        e = jnp.exp(s - top)
        total = jnp.sum(e, axis=-1, keepdims=True)
        lse = top + jnp.log(total)
        p = e / total
        out = mm(p.astype(BF), v)
        larger = jnp.maximum(lse, dense_lse)
        dense_part = jnp.exp(dense_lse - larger)
        own_part = jnp.exp(lse - larger)
        both = dense_part + own_part
        dense_part = dense_part / both
        own_part = own_part / both
        delta = dense_part * dense_dot + own_part * jnp.sum(gf * out, axis=-1, keepdims=True)
        p = p * own_part
        ds = (p * (mm_nt(gm, v) - delta) * SCALE).astype(BF)
        outs[0] = outs[0] + jnp.where(mine, mm(ds, k), 0.0)
        outs[1] = outs[1] + mm_tn(ds, qm)
        outs[2] = outs[2] + mm_tn(p.astype(BF), gm)
        outs[3] = outs[3] + jnp.where(mine, out * own_part, 0.0)
        columns[0] += list(split3(dense_part))
        columns[1] += list(split3(delta))
    outs[0] = put_scalars(outs[0], columns[0])
    outs[1] = put_scalars(outs[1], columns[1])
    for a in range(4):
        result = outs[a].astype(BF)
        for i in range(N_SEG):
            reply_ref[i, a] = result[SLAB * i : SLAB * (i + 1)]


def join_kernel(
    reply_ref, packed_ref, g_ref, soft_ref, back_ref,
    blended_ref, packed_grad_out, mine_ref, theirs_ref,
):
    small = head_mask(SLAB)
    shape = (ROWS, D)
    sampled = (iota(shape, 1) // HEAD) % RATE == iota(shape, 0) // SLAB

    def placed(a):
        row = jnp.concatenate(
            [reply_ref[j, a].astype(F32)[:, :BLOCK] for j in range(N_SEG)], axis=1
        )
        return jnp.where(sampled, jnp.concatenate([row] * RATE, axis=0), 0.0)

    def scalars(a, group):
        columns = []
        for h in range(GROUP * group, GROUP * (group + 1)):
            x = reply_ref[h // 2, a].astype(F32)
            at = BLOCK + 3 * (h % 2)
            columns.append(x[:, at : at + 1] + x[:, at + 1 : at + 2] + x[:, at + 2 : at + 3])
        return jnp.concatenate(columns, axis=0)

    parts = [[], [], [], []]
    for group in range(2):
        lanes = slice(group * WIDE, (group + 1) * WIDE)
        share, delta = scalars(0, group), scalars(1, group)
        q = jnp.where(small, stack_slabs(packed_ref[:, :D], group).astype(F32), 0.0).astype(BF)
        gm = jnp.where(small, stack_slabs(g_ref[...], group).astype(F32), 0.0).astype(BF)
        k = packed_ref[:, D + group * WIDE : D + (group + 1) * WIDE]
        p = soft_ref[group, 0] * share
        ds = (p * (soft_ref[group, 1] - delta) * SCALE).astype(BF)
        parts[0].append(back_ref[0, :, lanes] + unstack_slabs(jnp.where(small, mm(ds, k), 0.0)))
        parts[1].append(back_ref[1, :, lanes] + mm_tn(ds, q))
        parts[2].append(back_ref[2, :, lanes] + mm_tn(p.astype(BF), gm))
        parts[3].append(unstack_slabs(jnp.where(small, share, 0.0)))
    whole = [jnp.concatenate(part, axis=1) for part in parts]
    out = back_ref[3]
    blended = jnp.where(sampled, whole[3] * out + placed(3), out).astype(BF)
    blended_ref[...] = blended
    theirs_ref[:, 2 * QKV_HALF :] = blended
    grads = []
    for a in range(3):
        grad = (whole[a] + placed(a)).astype(BF)
        packed_grad_out.put(grad, slice(None), slice(a * D, (a + 1) * D))
        grads.append(grad.astype(F32))
    packed_grad_out.send(slice(None))
    grads = jnp.concatenate(grads, axis=1)
    mine, theirs = by_owner(grads, 72, QKV_HALF)
    mine_ref[...] = mine
    theirs_ref[:, : 2 * QKV_HALF] = theirs


def finish_kernel(
    length_ref, blended_ref, w_out_ref, packed_grad_ref, w_qkv_ref, xhat_ref,
    layer_ref, token_grad_ref, done_ref,
):
    length = length_ref[0]
    base = seg_index() * ROWS
    order = regroup()
    live = (base + place_of(iota((ROWS, 1), 0))) < length
    layer = jnp.where(live, mm(blended_ref[...], w_out_ref[...]), 0.0).astype(BF)
    layer_ref[0] = mm_tn(order, layer).astype(BF)
    dn = mm_nt(packed_grad_ref[...], w_qkv_ref[...])
    xhat = xhat_ref[:, :D]
    mean = jnp.mean(dn, axis=-1, keepdims=True)
    slope = jnp.mean(dn * xhat, axis=-1, keepdims=True)
    dx = ((dn - mean - xhat * slope) * xhat_ref[:, D : D + 1]).astype(BF)
    token_grad_ref[0] = mm_tn(order, dx).astype(BF)
    done_ref[...] = jnp.zeros(done_ref.shape, F32)


def weight_kernel(own_early_ref, early_ref, blended_ref, late_ref, mine_ref, partial_out):
    def both(own, other):
        return jnp.concatenate([own, other], axis=0)

    normed = both(own_early_ref[:, 4 * OUT_HALF :], early_ref[:, 4 * OUT_HALF :])
    blended = both(blended_ref[...], late_ref[:, 2 * QKV_HALF :])
    for half in range(2):
        at = half * QKV_HALF
        qkv = mm_tn(normed, both(mine_ref[:, at : at + 576], late_ref[:, at : at + 576]))
        at = half * OUT_HALF
        out = mm_tn(
            blended,
            both(
                own_early_ref[:, 2 * OUT_HALF + at : 2 * OUT_HALF + at + 192],
                early_ref[:, at : at + 192],
            ),
        )
        for xl in range(2):
            total = jnp.concatenate(
                [
                    qkv[:, 288 * xl : 288 * (xl + 1)],
                    out[:, BLOCK * xl : BLOCK * (xl + 1)],
                ],
                axis=1,
            ).astype(BF)
            for s in range(N_SEG):
                lanes = slice(half * WIDE, (half + 1) * WIDE)
                rows = total[BLOCK * s : BLOCK * (s + 1)]
                partial_out.put(rows, N_SEG * xl + s, slice(None), lanes)
            partial_out.send(slice(N_SEG * xl, N_SEG * (xl + 1)), slice(None), lanes)


def plane_sum_kernel(parts_ref, out_ref):
    for half in range(2):
        lanes = slice(half * WIDE, (half + 1) * WIDE)
        total = parts_ref[0, :, lanes].astype(F32)
        for n in range(1, 16):
            total = total + parts_ref[n, :, lanes].astype(F32)
        for z in range(4):
            out_ref[4 * half + z] = jnp.concatenate(
                [total[:, 72 * z : 72 * z + 72], total[:, 288 + 24 * z : 312 + 24 * z]], axis=1
            ).astype(BF)


def last_sum_kernel(parts_ref, in_ref, out_ref):
    total = parts_ref[0].astype(F32)
    for z in range(1, 8):
        total = total + parts_ref[z].astype(F32)
    total = total.T
    in_ref[...] = total[:72]
    out_ref[...] = total[72:]


class Held:
    def __init__(self, source, target, sem):
        self.target = target
        self.copy = pltpu.make_async_copy(source, target, sem)
        self.copy.start()
        self.here = False

    def __getitem__(self, index):
        if not self.here:
            self.copy.wait()
            self.here = True
        return self.target[index]


class Sent:
    def __init__(self, slot, target, sems, parts):
        self.slot, self.target, self.sems, self.parts = slot, target, sems, parts
        self.copies = []

    def put(self, value, *index):
        index = index or (slice(None),)
        self.slot[index] = value
        if self.parts == 1:
            self.send(*index)

    def send(self, *index):
        copy = pltpu.make_async_copy(
            self.slot.at[index], self.target.at[index], self.sems[len(self.copies)]
        )
        copy.start()
        self.copies.append(copy)


def call(kernel, outs, *inputs):
    specs = {"s": SMEM, "v": VMEM, "f": ANY, "h": ANY, "n": ANY}
    kinds = [kind for kind, _ in inputs]
    arrays = [
        pltpu.with_memory_space_constraint(x, pltpu.HBM) if kind == "h" else x
        for kind, x in inputs
    ]
    moved = [x for kind, x in inputs if kind in "fh"]
    count = len(moved) + sum(out[2] for out in outs if len(out) > 2)
    moved += [jax.ShapeDtypeStruct(*out[:2]) for out in outs if len(out) > 2]

    def body(*refs):
        n, m = len(kinds), len(outs)
        slots = list(refs[n + m : -1]) if moved else []
        sems = [refs[-1].at[i] for i in range(count)]
        given, sent = [], []
        for kind, ref in zip(kinds, refs[:n]):
            if kind in "fh":
                given.append(Held(ref, slots.pop(0), sems.pop(0)))
            elif kind != "n":
                given.append(ref)
        for out, ref in zip(outs, refs[n : n + m]):
            if len(out) > 2:
                ref = Sent(slots.pop(0), ref, [sems.pop(0) for _ in range(out[2])], out[2])
                sent.append(ref)
            given.append(ref)
        kernel(*given)
        for ref in sent:
            for copy in ref.copies:
                copy.wait()

    scratch = [pltpu.VMEM(x.shape, x.dtype) for x in moved]
    if moved:
        scratch.append(pltpu.SemaphoreType.DMA((count,)))
    return pl.pallas_call(
        body,
        out_shape=[
            pltpu.HBM(*out[:2]) if len(out) > 2 else jax.ShapeDtypeStruct(*out) for out in outs
        ],
        in_specs=[specs[kind] for kind in kinds],
        out_specs=[ANY if len(out) > 2 else VMEM for out in outs],
        scratch_shapes=scratch,
        compiler_params=pltpu.CompilerParams(vmem_limit_bytes=LIMIT),
        name=kernel.__name__,
    )(*arrays)


def to_core(x):
    return lax.ppermute(x, "core", [(0, 1), (1, 0)])


def per_device(tokens, coords, lengths, w_qkv, w_out, cotangent):
    message, packed, g, xhat, out_grad = call(
        first_kernel,
        [
            ((N_SEG, 4, SLAB, 128), BF),
            ((ROWS, 3 * D), BF),
            ((ROWS, D), BF),
            ((ROWS, D + 128), F32, 1),
            ((ROWS, D), BF, 1),
        ],
        ("s", lengths),
        ("h", jnp.transpose(coords, (0, 2, 1))),
        ("h", cotangent),
        ("h", tokens),
        ("h", w_out),
        ("h", w_qkv),
    )
    message = lax.all_to_all(message, ("xh", "y"), 0, 0, tiled=True)
    back, soft, own_early = call(
        dense_kernel,
        [
            ((4, ROWS, D), F32),
            ((2, 2, GROUP * SLAB, ROWS), F32),
            ((ROWS, 4 * OUT_HALF + D), BF),
        ],
        ("s", lengths),
        ("v", packed),
        ("v", g),
        ("h", xhat),
        ("h", out_grad),
    )
    (reply,) = call(
        dilated_kernel,
        [((N_SEG, 4, SLAB, 128), BF)],
        ("s", lengths),
        ("v", message),
        ("n", soft),
    )
    reply = lax.all_to_all(reply, ("xh", "y"), 0, 0, tiled=True)
    early = to_core(own_early)
    blended, packed_grad, mine, late = call(
        join_kernel,
        [
            ((ROWS, D), BF),
            ((ROWS, 3 * D), BF, 2),
            ((ROWS, 2 * QKV_HALF), BF),
            ((ROWS, 2 * QKV_HALF + D), BF),
        ],
        ("v", reply),
        ("v", packed),
        ("h", g),
        ("v", soft),
        ("v", back),
        ("n", early),
    )
    late = to_core(late)
    (partial,) = call(
        weight_kernel,
        [((16, BLOCK, D), BF, 4)],
        ("v", own_early),
        ("v", early),
        ("v", blended),
        ("v", late),
        ("v", mine),
    )
    partial = lax.all_to_all(partial, ("xl", "xh", "y"), 0, 0, tiled=True)
    layer_out, token_grad, done = call(
        finish_kernel,
        [((1, ROWS, D), BF), ((1, ROWS, D), BF), ((8, 128), F32)],
        ("s", lengths),
        ("f", blended),
        ("h", w_out),
        ("h", packed_grad),
        ("h", w_qkv),
        ("h", xhat),
    )
    (partial,) = call(
        plane_sum_kernel, [((8, BLOCK, BLOCK), BF)], ("v", partial), ("n", done)
    )
    arrived = lax.all_to_all(partial, "z", 0, 0, tiled=True)
    grad_in, grad_out = call(
        last_sum_kernel, [((72, BLOCK), F32), ((24, BLOCK), F32)], ("v", arrived)
    )
    return layer_out, token_grad, grad_in.T, grad_out.T


def solution(mesh):
    devices = mesh.devices.reshape(8, 2, 2, 2, 4)
    fine = Mesh(devices, ("z", "xl", "core", "xh", "y"))
    dp, seg = ("z", "xl", "core"), ("xh", "y")
    placed = (P(dp, seg, None), P(dp, seg, None), P(dp), P(), P(), P(dp, seg, None))
    return jax.shard_map(
        per_device,
        mesh=fine,
        in_specs=placed,
        out_specs=(P(dp, seg, None), P(dp, seg, None), P(seg, dp), P(seg, dp)),
        check_vma=False,
    )
```

```python
import functools

import jax
import jax.numpy as jnp
from jax import lax
from jax.experimental import pallas as pl
from jax.experimental.pallas import tpu as pltpu
from jax.sharding import Mesh
from jax.sharding import PartitionSpec as P

HEADS = 16
RATE = 4
HEAD = 48
GROUP = 8
WIDE = GROUP * HEAD
ROWS = 128
SLAB = ROWS // RATE
D = 768
N_SEG = 8
BLOCK = 96
QKV_HALF = 640
OUT_HALF = 256
EPSILON = 1e-05
NEG_FILL = -1e30
SCALE = HEAD ** (-0.5)
BF = jnp.bfloat16
F32 = jnp.float32
VMEM = pl.BlockSpec(memory_space=pltpu.VMEM)
SMEM = pl.BlockSpec(memory_space=pltpu.SMEM)
ANY = pl.BlockSpec(memory_space=pl.ANY)
LIMIT = 20 * 1024 * 1024


def iota(shape, dim):
    return lax.broadcasted_iota(jnp.int32, shape, dim)


def mm(a, b):
    return lax.dot_general(a, b, (((1,), (0,)), ((), ())), preferred_element_type=F32)


def mm_nt(a, b):
    return lax.dot_general(a, b, (((1,), (1,)), ((), ())), preferred_element_type=F32)


def mm_tn(a, b):
    return lax.dot_general(a, b, (((0,), (0,)), ((), ())), preferred_element_type=F32)


def regroup():
    row, col = iota((ROWS, ROWS), 0), iota((ROWS, ROWS), 1)
    return (col == RATE * (row % SLAB) + row // SLAB).astype(BF)


def place_of(row):
    return RATE * (row % SLAB) + row // SLAB


def sin_cos_code(c0, c1):
    quarter = D // 4
    col = iota((1, D), 1)
    block = col // quarter
    freqs = jnp.exp((-jnp.log(F32(10000.0))) * (col - block * quarter).astype(F32) / quarter)
    angle = jnp.where(block < 2, c0, c1) * freqs
    turns = jnp.floor(angle * F32(0.6366197723675814) + F32(0.5))
    rest = angle - turns * F32(1.5703125)
    rest = rest - turns * F32(4.837512969970703e-4)
    rest = rest - turns * F32(7.549789948768648e-8)
    sq = rest * rest
    sine = rest + rest * sq * (
        F32(-1.6666654611e-1) + sq * (F32(8.3321608736e-3) + sq * F32(-1.9515295891e-4))
    )
    cosine = (
        F32(1.0)
        - F32(0.5) * sq
        + sq * sq * (F32(4.166664568298827e-2) + sq * (F32(-1.388731625493765e-3) + sq * F32(2.443315711809948e-5)))
    )
    quadrant = turns.astype(jnp.int32) + (block & 1)
    value = jnp.where((quadrant & 1) == 1, cosine, sine)
    return jnp.where((quadrant & 2) == 2, -value, value)


def head_mask(rows_per_head):
    shape = (GROUP * rows_per_head, WIDE)
    return iota(shape, 0) // rows_per_head == iota(shape, 1) // HEAD


def split3(x):
    hi = x.astype(BF)
    rest = x - hi.astype(F32)
    mid = rest.astype(BF)
    lo = (rest - mid.astype(F32)).astype(BF)
    return hi, mid, lo


def put_scalars(base, columns):
    lane = iota(base.shape, 1)
    for n, column in enumerate(columns):
        base = jnp.where(lane == BLOCK + n, column.astype(F32), base)
    return base


def stack_slabs(array, group):
    part = array[:, group * WIDE : (group + 1) * WIDE]
    return jnp.concatenate(
        [part[SLAB * (h % RATE) : SLAB * (h % RATE) + SLAB] for h in range(GROUP)], axis=0
    )


def unstack_slabs(stack):
    return jnp.concatenate(
        [
            stack[SLAB * o : SLAB * o + SLAB] + stack[SLAB * (o + RATE) : SLAB * (o + RATE) + SLAB]
            for o in range(RATE)
        ],
        axis=0,
    )


def seg_index():
    return lax.axis_index("xh") * 4 + lax.axis_index("y")


def first_kernel(
    length_ref, coord_ref, cot_ref, tok_ref, w_out_ref, w_qkv_ref,
    message_ref, packed_ref, g_ref, xhat_out, out_grad_out,
):
    length = length_ref[0]
    base = seg_index() * ROWS
    order = regroup()
    coords = coord_ref[0].astype(F32).astype(BF)
    cotangent, tokens, w_out = cot_ref[0], tok_ref[0], w_out_ref[...]
    live = (base + place_of(iota((ROWS, 1), 0))) < length
    out_grad = jnp.where(live, mm(order, cotangent), 0.0).astype(BF)
    out_grad_out.put(out_grad)
    g = mm_nt(out_grad, w_out).astype(BF)
    g_ref[...] = g
    coords = mm_nt(order, coords)
    embedded = mm(order, tokens) + sin_cos_code(coords[:, 0:1], coords[:, 1:2])
    centred = embedded - jnp.mean(embedded, axis=-1, keepdims=True)
    rstd = lax.rsqrt(jnp.mean(centred * centred, axis=-1, keepdims=True) + EPSILON)
    xhat = centred * rstd
    xhat_out.put(jnp.concatenate([xhat, jnp.broadcast_to(rstd, (ROWS, 128))], axis=1))
    packed = mm(xhat.astype(BF), w_qkv_ref[...]).astype(BF)
    packed_ref[...] = packed

    mask = head_mask(SLAB)
    key_col = place_of(iota((1, ROWS), 1))
    row = iota((GROUP * SLAB, 1), 0)
    query_col = RATE * (row % SLAB) + (row // SLAB) % RATE
    allowed = jnp.logical_or(base + key_col < length, key_col == query_col)
    scalars = []
    for group in range(2):
        q = jnp.where(mask, stack_slabs(packed[:, :D], group).astype(F32), 0.0).astype(BF)
        gs = stack_slabs(g, group).astype(F32)
        k = packed[:, D + group * WIDE : D + (group + 1) * WIDE]
        v = packed[:, 2 * D + group * WIDE : 2 * D + (group + 1) * WIDE]
        s = jnp.where(allowed, mm_nt(q, k) * SCALE, NEG_FILL)
        top = jnp.max(s, axis=-1, keepdims=True)
        e = jnp.exp(s - top)
        total = jnp.sum(e, axis=-1, keepdims=True)
        lse = top + jnp.log(total)
        out = mm((e / total).astype(BF), v)
        g_dot = jnp.sum(jnp.where(mask, gs * out, 0.0), axis=-1, keepdims=True)
        scalars.append((lse, g_dot))

    lane = iota((SLAB, BLOCK), 1)
    pad = jnp.zeros((SLAB, 128 - BLOCK), F32)
    for j in range(N_SEG):
        r0 = SLAB * ((2 * j) % RATE)
        columns = [[], []]
        for h in (2 * j, 2 * j + 1):
            at = (h % GROUP) * SLAB
            for which in range(2):
                columns[which] += list(split3(scalars[h // GROUP][which][at : at + SLAB]))
        for a in range(4):
            if a < 3:
                part = packed[r0 : r0 + 2 * SLAB, a * D + BLOCK * j : a * D + BLOCK * (j + 1)]
            else:
                part = g[r0 : r0 + 2 * SLAB, BLOCK * j : BLOCK * (j + 1)]
            part = part.astype(F32)
            part = jnp.where(lane < HEAD, part[:SLAB], part[SLAB:])
            part = jnp.concatenate([part, pad], axis=1)
            if a < 2:
                part = put_scalars(part, columns[a])
            message_ref[j, a] = part.astype(BF)


def by_owner(array, width, padded):
    pad = jnp.zeros((ROWS, padded - 8 * width), array.dtype)
    sides = []
    for c in range(2):
        pieces = []
        for z_hi in range(2):
            for xl in range(2):
                for z_lo in range(4):
                    dp = (z_hi * 4 + z_lo) * 4 + xl * 2 + c
                    pieces.append(array[:, width * dp : width * (dp + 1)])
            pieces.append(pad)
        sides.append(jnp.concatenate(pieces, axis=1).astype(BF))
    first = lax.axis_index("core") == 0
    return jnp.where(first, sides[0], sides[1]), jnp.where(first, sides[1], sides[0])


def dense_kernel(
    length_ref, packed_ref, g_ref, xhat_ref, out_grad_ref,
    back_ref, soft_ref, early_ref,
):
    length = length_ref[0]
    base = seg_index() * ROWS
    mask = head_mask(ROWS)
    row = iota((GROUP * ROWS, 1), 0)
    key_col = place_of(iota((1, ROWS), 1))
    query_col = place_of(row % ROWS)
    allowed = jnp.logical_or(base + key_col < length, key_col == query_col)
    free = (row % ROWS) // SLAB != (row // ROWS) % RATE

    def spread(part):
        return jnp.where(mask, jnp.concatenate([part.astype(F32)] * GROUP, axis=0), 0.0)

    def fold(stack):
        stack = jnp.where(mask, stack, 0.0)
        return sum(stack[ROWS * h : ROWS * (h + 1)] for h in range(GROUP))

    for group in range(2):
        lanes = slice(group * WIDE, (group + 1) * WIDE)
        q = spread(packed_ref[:, group * WIDE : (group + 1) * WIDE]).astype(BF)
        k = packed_ref[:, D + group * WIDE : D + (group + 1) * WIDE]
        v = packed_ref[:, 2 * D + group * WIDE : 2 * D + (group + 1) * WIDE]
        gm = spread(g_ref[:, lanes])
        gb = gm.astype(BF)
        s = jnp.where(allowed, mm_nt(q, k) * SCALE, NEG_FILL)
        e = jnp.exp(s - jnp.max(s, axis=-1, keepdims=True))
        p = e / jnp.sum(e, axis=-1, keepdims=True)
        out = mm(p.astype(BF), v)
        delta = jnp.sum(gm * out, axis=-1, keepdims=True)
        dp = mm_nt(gb, v)
        back_ref[3, :, lanes] = fold(out)
        free_p = jnp.where(free, p, 0.0)
        ds = (free_p * (dp - delta) * SCALE).astype(BF)
        back_ref[0, :, lanes] = fold(mm(ds, k))
        back_ref[1, :, lanes] = mm_tn(ds, q)
        back_ref[2, :, lanes] = mm_tn(free_p.astype(BF), gb)
        for h in range(GROUP):
            at = ROWS * h + SLAB * (h % RATE)
            to = slice(SLAB * h, SLAB * (h + 1))
            soft_ref[group, 0, to] = p[at : at + SLAB]
            soft_ref[group, 1, to] = dp[at : at + SLAB]
    mine, theirs = by_owner(out_grad_ref[...].astype(F32), 24, OUT_HALF)
    early_ref[:, : 2 * OUT_HALF] = theirs
    early_ref[:, 2 * OUT_HALF : 4 * OUT_HALF] = mine
    early_ref[:, 4 * OUT_HALF :] = xhat_ref[:, :D].astype(BF)


def dilated_kernel(length_ref, message_ref, reply_ref):
    length = length_ref[0]
    j = seg_index()
    n = N_SEG * SLAB
    stack = []
    for a in range(4):
        stack.append(jnp.concatenate([message_ref[i, a] for i in range(N_SEG)], axis=0))
    q, k, v, g = stack
    lane = iota((n, 128), 1)
    scalar_lane = q.astype(F32), k.astype(F32)
    key = iota((1, n), 1)
    query = iota((n, 1), 0)
    outs = [jnp.zeros((n, 128), F32) for _ in range(4)]
    columns = [[], []]
    for half in range(2):
        mine = jnp.logical_and(lane >= HEAD * half, lane < HEAD * (half + 1))
        offset = (2 * j + half) % RATE

        def scalar(which):
            at = BLOCK + 3 * half
            x = scalar_lane[which]
            return x[:, at : at + 1] + x[:, at + 1 : at + 2] + x[:, at + 2 : at + 3]

        dense_lse, dense_dot = scalar(0), scalar(1)
        qm = jnp.where(mine, q.astype(F32), 0.0).astype(BF)
        gf = jnp.where(mine, g.astype(F32), 0.0)
        gm = gf.astype(BF)
        allowed = jnp.logical_or(RATE * key + offset < length, key == query)
        s = jnp.where(allowed, mm_nt(qm, k) * SCALE, NEG_FILL)
        top = jnp.max(s, axis=-1, keepdims=True)
        e = jnp.exp(s - top)
        total = jnp.sum(e, axis=-1, keepdims=True)
        lse = top + jnp.log(total)
        p = e / total
        out = mm(p.astype(BF), v)
        larger = jnp.maximum(lse, dense_lse)
        dense_part = jnp.exp(dense_lse - larger)
        own_part = jnp.exp(lse - larger)
        both = dense_part + own_part
        dense_part = dense_part / both
        own_part = own_part / both
        delta = dense_part * dense_dot + own_part * jnp.sum(gf * out, axis=-1, keepdims=True)
        p = p * own_part
        ds = (p * (mm_nt(gm, v) - delta) * SCALE).astype(BF)
        outs[0] = outs[0] + jnp.where(mine, mm(ds, k), 0.0)
        outs[1] = outs[1] + mm_tn(ds, qm)
        outs[2] = outs[2] + mm_tn(p.astype(BF), gm)
        outs[3] = outs[3] + jnp.where(mine, out * own_part, 0.0)
        columns[0] += list(split3(dense_part))
        columns[1] += list(split3(delta))
    outs[0] = put_scalars(outs[0], columns[0])
    outs[1] = put_scalars(outs[1], columns[1])
    for a in range(4):
        result = outs[a].astype(BF)
        for i in range(N_SEG):
            reply_ref[i, a] = result[SLAB * i : SLAB * (i + 1)]


def join_kernel(
    reply_ref, packed_ref, g_ref, soft_ref, back_ref,
    blended_ref, packed_grad_ref, mine_ref, theirs_ref,
):
    small = head_mask(SLAB)
    shape = (ROWS, D)
    sampled = (iota(shape, 1) // HEAD) % RATE == iota(shape, 0) // SLAB

    def placed(a):
        row = jnp.concatenate(
            [reply_ref[j, a].astype(F32)[:, :BLOCK] for j in range(N_SEG)], axis=1
        )
        return jnp.where(sampled, jnp.concatenate([row] * RATE, axis=0), 0.0)

    def scalars(a, group):
        columns = []
        for h in range(GROUP * group, GROUP * (group + 1)):
            x = reply_ref[h // 2, a].astype(F32)
            at = BLOCK + 3 * (h % 2)
            columns.append(x[:, at : at + 1] + x[:, at + 1 : at + 2] + x[:, at + 2 : at + 3])
        return jnp.concatenate(columns, axis=0)

    parts = [[], [], [], []]
    for group in range(2):
        lanes = slice(group * WIDE, (group + 1) * WIDE)
        share, delta = scalars(0, group), scalars(1, group)
        q = jnp.where(small, stack_slabs(packed_ref[:, :D], group).astype(F32), 0.0).astype(BF)
        gm = jnp.where(small, stack_slabs(g_ref[...], group).astype(F32), 0.0).astype(BF)
        k = packed_ref[:, D + group * WIDE : D + (group + 1) * WIDE]
        p = soft_ref[group, 0] * share
        ds = (p * (soft_ref[group, 1] - delta) * SCALE).astype(BF)
        parts[0].append(back_ref[0, :, lanes] + unstack_slabs(jnp.where(small, mm(ds, k), 0.0)))
        parts[1].append(back_ref[1, :, lanes] + mm_tn(ds, q))
        parts[2].append(back_ref[2, :, lanes] + mm_tn(p.astype(BF), gm))
        parts[3].append(unstack_slabs(jnp.where(small, share, 0.0)))
    whole = [jnp.concatenate(part, axis=1) for part in parts]
    out = back_ref[3]
    blended = jnp.where(sampled, whole[3] * out + placed(3), out).astype(BF)
    blended_ref[...] = blended
    theirs_ref[:, 2 * QKV_HALF :] = blended
    grads = []
    for a in range(3):
        grad = (whole[a] + placed(a)).astype(BF)
        packed_grad_ref[:, a * D : (a + 1) * D] = grad
        grads.append(grad.astype(F32))
    grads = jnp.concatenate(grads, axis=1)
    mine, theirs = by_owner(grads, 72, QKV_HALF)
    mine_ref[...] = mine
    theirs_ref[:, : 2 * QKV_HALF] = theirs


def finish_kernel(
    length_ref, blended_ref, w_out_ref, packed_grad_ref, w_qkv_ref, xhat_ref,
    layer_ref, token_grad_ref, done_ref,
):
    length = length_ref[0]
    base = seg_index() * ROWS
    order = regroup()
    live = (base + place_of(iota((ROWS, 1), 0))) < length
    layer = jnp.where(live, mm(blended_ref[...], w_out_ref[...]), 0.0).astype(BF)
    layer_ref[0] = mm_tn(order, layer).astype(BF)
    dn = mm_nt(packed_grad_ref[...], w_qkv_ref[...])
    xhat = xhat_ref[:, :D]
    mean = jnp.mean(dn, axis=-1, keepdims=True)
    slope = jnp.mean(dn * xhat, axis=-1, keepdims=True)
    dx = ((dn - mean - xhat * slope) * xhat_ref[:, D : D + 1]).astype(BF)
    token_grad_ref[0] = mm_tn(order, dx).astype(BF)
    done_ref[...] = jnp.zeros(done_ref.shape, F32)


def weight_kernel(
    half, own_early_ref, early_ref, blended_ref, late_ref, mine_ref, out_ref
):
    xh, xl, y = lax.axis_index("xh"), lax.axis_index("xl"), lax.axis_index("y")
    core = lax.axis_index("core")

    def both(own, other):
        return jnp.concatenate([own, other], axis=0)

    at = half * QKV_HALF
    qkv = mm_tn(
        both(own_early_ref[:, 4 * OUT_HALF :], early_ref[:, 4 * OUT_HALF :]),
        both(mine_ref[:, at : at + 576], late_ref[:, at : at + 576]),
    ).astype(BF)
    at = half * OUT_HALF
    out = mm_tn(
        both(blended_ref[...], late_ref[:, 2 * QKV_HALF :]),
        both(
            own_early_ref[:, 2 * OUT_HALF + at : 2 * OUT_HALF + at + 192],
            early_ref[:, at : at + 192],
        ),
    ).astype(BF)
    for to_xl in range(2):
        total = jnp.concatenate(
            [
                qkv[:, 288 * to_xl : 288 * (to_xl + 1)].astype(F32),
                out[:, BLOCK * to_xl : BLOCK * (to_xl + 1)].astype(F32),
            ],
            axis=1,
        ).astype(BF)
        for s in range(N_SEG):
            x_rel = 2 * ((s // 4 + xh) % 2) + (to_xl + xl) % 2
            y_rel = (s % 4 - y + 4) % 4
            first = jnp.where(core == 0, y_rel, x_rel)
            second = jnp.where(core == 0, x_rel, y_rel)
            out_ref[first, second] = total[BLOCK * s : BLOCK * (s + 1)]


def first_sum_kernel(*refs):
    out_ref = refs[-1]
    for half in range(2):
        own_ref, a_ref, b_ref, c_ref = refs[4 * half : 4 * half + 4]
        for k in range(4):
            total = own_ref[0, k].astype(F32) + a_ref[k].astype(F32)
            total = total + (b_ref[k].astype(F32) + c_ref[k].astype(F32))
            out_ref[k, :, half * WIDE : (half + 1) * WIDE] = total.astype(BF)


def second_sum_kernel(own_ref, a_ref, b_ref, c_ref, out_ref):
    whole = own_ref[0].astype(F32) + a_ref[...].astype(F32)
    whole = whole + (b_ref[...].astype(F32) + c_ref[...].astype(F32))
    for half in range(2):
        total = whole[:, half * WIDE : (half + 1) * WIDE]
        for z in range(4):
            piece = jnp.concatenate(
                [total[:, 72 * z : 72 * z + 72], total[:, 288 + 24 * z : 312 + 24 * z]], axis=1
            )
            side = jnp.concatenate([piece[72:, 32 * n : 32 * n + 32] for n in range(3)], axis=0)
            out_ref[4 * half + z] = jnp.concatenate([piece[:72], side], axis=1).astype(BF)


def last_sum_kernel(parts_ref, in_ref, out_ref):
    total = parts_ref[0].astype(F32)
    for z in range(1, 8):
        total = total + parts_ref[z].astype(F32)
    side = total[:, BLOCK:]
    foot = jnp.concatenate([side[24 * n : 24 * n + 24] for n in range(3)], axis=1)
    total = jnp.concatenate([total[:, :BLOCK], foot], axis=0).T
    in_ref[...] = total[:72]
    out_ref[...] = total[72:]


class Held:
    def __init__(self, source, target, sem):
        self.target = target
        self.copy = pltpu.make_async_copy(source, target, sem)
        self.copy.start()
        self.here = False

    def __getitem__(self, index):
        if not self.here:
            self.copy.wait()
            self.here = True
        return self.target[index]


class Sent:
    def __init__(self, slot, target, sem):
        self.slot = slot
        self.copy = pltpu.make_async_copy(slot, target, sem)

    def put(self, value):
        self.slot[...] = value
        self.copy.start()


def call(kernel, outs, *inputs):
    specs = {"s": SMEM, "v": VMEM, "f": ANY, "h": ANY, "n": ANY}
    kinds = [kind for kind, _ in inputs]
    arrays = [
        pltpu.with_memory_space_constraint(x, pltpu.HBM) if kind == "h" else x
        for kind, x in inputs
    ]
    moved = [x for kind, x in inputs if kind in "fh"]
    moved += [jax.ShapeDtypeStruct(*out[:2]) for out in outs if len(out) > 2]

    def body(*refs):
        n, m = len(kinds), len(outs)
        slots = list(refs[n + m : -1]) if moved else []
        given, sent = [], []
        for kind, ref in zip(kinds, refs[:n]):
            if kind in "fh":
                given.append(Held(ref, slots.pop(0), refs[-1].at[len(slots)]))
            elif kind != "n":
                given.append(ref)
        for out, ref in zip(outs, refs[n : n + m]):
            if len(out) > 2:
                ref = Sent(slots.pop(0), ref, refs[-1].at[len(slots)])
                sent.append(ref)
            given.append(ref)
        kernel(*given)
        for ref in sent:
            ref.copy.wait()

    scratch = [pltpu.VMEM(x.shape, x.dtype) for x in moved]
    if moved:
        scratch.append(pltpu.SemaphoreType.DMA((len(moved),)))
    return pl.pallas_call(
        body,
        out_shape=[
            pltpu.HBM(*out[:2]) if len(out) > 2 else jax.ShapeDtypeStruct(*out) for out in outs
        ],
        in_specs=[specs[kind] for kind in kinds],
        out_specs=[ANY if len(out) > 2 else VMEM for out in outs],
        scratch_shapes=scratch,
        compiler_params=pltpu.CompilerParams(vmem_limit_bytes=LIMIT),
        name=kernel.__name__,
    )(*arrays)


def named(name, kernel):
    def run(*refs):
        kernel(*refs)

    run.__name__ = name
    return run


def to_core(x):
    return lax.ppermute(x, "core", [(0, 1), (1, 0)])


def swap(x, k, stage):
    pairs = []
    for i in range(32):
        xl, core, xh, y = i // 16, (i // 8) % 2, (i // 4) % 2, i % 4
        if core == stage:
            y = (y + k) % 4
        else:
            xl, xh = xl ^ (k % 2), xh ^ (k // 2)
        pairs.append((i, ((xl * 2 + core) * 2 + xh) * 4 + y))
    return lax.ppermute(x, ("xl", "core", "xh", "y"), pairs)


def per_device(tokens, coords, lengths, w_qkv, w_out, cotangent):
    message, packed, g, xhat, out_grad = call(
        first_kernel,
        [
            ((N_SEG, 4, SLAB, 128), BF),
            ((ROWS, 3 * D), BF),
            ((ROWS, D), BF),
            ((ROWS, D + 128), F32, "h"),
            ((ROWS, D), BF, "h"),
        ],
        ("s", lengths),
        ("h", jnp.transpose(coords, (0, 2, 1))),
        ("h", cotangent),
        ("h", tokens),
        ("h", w_out),
        ("h", w_qkv),
    )
    message = lax.all_to_all(message, ("xh", "y"), 0, 0, tiled=True)
    back, soft, own_early = call(
        dense_kernel,
        [
            ((4, ROWS, D), F32),
            ((2, 2, GROUP * SLAB, ROWS), F32),
            ((ROWS, 4 * OUT_HALF + D), BF),
        ],
        ("s", lengths),
        ("v", packed),
        ("v", g),
        ("h", xhat),
        ("h", out_grad),
    )
    (reply,) = call(
        dilated_kernel,
        [((N_SEG, 4, SLAB, 128), BF)],
        ("s", lengths),
        ("v", message),
        ("n", soft),
    )
    reply = lax.all_to_all(reply, ("xh", "y"), 0, 0, tiled=True)
    early = to_core(own_early)
    blended, packed_grad, mine, late = call(
        join_kernel,
        [
            ((ROWS, D), BF),
            ((ROWS, 3 * D), BF),
            ((ROWS, 2 * QKV_HALF), BF),
            ((ROWS, 2 * QKV_HALF + D), BF),
        ],
        ("v", reply),
        ("v", packed),
        ("v", g),
        ("v", soft),
        ("v", back),
        ("n", early),
    )
    late = to_core(late)
    halves = []
    for half in range(2):
        (partial,) = call(
            named("weight_kernel", functools.partial(weight_kernel, half)),
            [((4, 4, BLOCK, WIDE), BF)],
            ("v", own_early),
            ("v", early),
            ("v", blended),
            ("v", late),
            ("v", mine),
        )
        halves.append(partial)
    layer_out, token_grad, done = call(
        finish_kernel,
        [((1, ROWS, D), BF), ((1, ROWS, D), BF), ((8, 128), F32)],
        ("s", lengths),
        ("f", blended),
        ("h", w_out),
        ("f", packed_grad),
        ("h", w_qkv),
        ("h", xhat),
    )
    terms = []
    for partial in halves:
        terms.append(("v", partial))
        terms += [("v", swap(partial[k], k, 0)) for k in (1, 3, 2)]
    (partial,) = call(first_sum_kernel, [((4, BLOCK, D), BF)], *terms, ("n", done))
    terms = [("v", swap(partial[k], k, 1)) for k in (1, 3, 2)]
    (partial,) = call(
        second_sum_kernel, [((8, 72, 128), BF)], ("v", partial), *terms
    )
    arrived = lax.all_to_all(partial, "z", 0, 0, tiled=True)
    grad_in, grad_out = call(
        last_sum_kernel, [((72, BLOCK), F32), ((24, BLOCK), F32)], ("v", arrived)
    )
    return layer_out, token_grad, grad_in.T, grad_out.T


def solution(mesh):
    devices = mesh.devices.reshape(8, 2, 2, 2, 4)
    fine = Mesh(devices, ("z", "xl", "core", "xh", "y"))
    dp, seg = ("z", "xl", "core"), ("xh", "y")
    placed = (P(dp, seg, None), P(dp, seg, None), P(dp), P(), P(), P(dp, seg, None))
    return jax.shard_map(
        per_device,
        mesh=fine,
        in_specs=placed,
        out_specs=(P(dp, seg, None), P(dp, seg, None), P(seg, dp), P(seg, dp)),
        check_vma=False,
    )
```

```python
import functools

import jax
import jax.numpy as jnp
from jax import lax
from jax.experimental import pallas as pl
from jax.experimental.pallas import tpu as pltpu
from jax.sharding import Mesh
from jax.sharding import PartitionSpec as P

HEADS = 16
RATE = 4
HEAD = 48
GROUP = 8
WIDE = GROUP * HEAD
ROWS = 128
SLAB = ROWS // RATE
D = 768
N_SEG = 8
BLOCK = 96
QKV_HALF = 640
OUT_HALF = 256
EPSILON = 1e-05
NEG_FILL = -1e30
SCALE = HEAD ** (-0.5)
BF = jnp.bfloat16
F32 = jnp.float32
VMEM = pl.BlockSpec(memory_space=pltpu.VMEM)
SMEM = pl.BlockSpec(memory_space=pltpu.SMEM)
ANY = pl.BlockSpec(memory_space=pl.ANY)
LIMIT = 20 * 1024 * 1024


def iota(shape, dim):
    return lax.broadcasted_iota(jnp.int32, shape, dim)


def mm(a, b):
    return lax.dot_general(a, b, (((1,), (0,)), ((), ())), preferred_element_type=F32)


def mm_nt(a, b):
    return lax.dot_general(a, b, (((1,), (1,)), ((), ())), preferred_element_type=F32)


def mm_tn(a, b):
    return lax.dot_general(a, b, (((0,), (0,)), ((), ())), preferred_element_type=F32)


def regroup():
    row, col = iota((ROWS, ROWS), 0), iota((ROWS, ROWS), 1)
    return (col == RATE * (row % SLAB) + row // SLAB).astype(BF)


def place_of(row):
    return RATE * (row % SLAB) + row // SLAB


def sin_cos_code(c0, c1):
    quarter = D // 4
    col = iota((1, D), 1)
    block = col // quarter
    freqs = jnp.exp((-jnp.log(F32(10000.0))) * (col - block * quarter).astype(F32) / quarter)
    angle = jnp.where(block < 2, c0, c1) * freqs
    turns = jnp.floor(angle * F32(0.6366197723675814) + F32(0.5))
    rest = angle - turns * F32(1.5703125)
    rest = rest - turns * F32(4.837512969970703e-4)
    rest = rest - turns * F32(7.549789948768648e-8)
    sq = rest * rest
    sine = rest + rest * sq * (
        F32(-1.6666654611e-1) + sq * (F32(8.3321608736e-3) + sq * F32(-1.9515295891e-4))
    )
    cosine = (
        F32(1.0)
        - F32(0.5) * sq
        + sq * sq * (F32(4.166664568298827e-2) + sq * (F32(-1.388731625493765e-3) + sq * F32(2.443315711809948e-5)))
    )
    quadrant = turns.astype(jnp.int32) + (block & 1)
    value = jnp.where((quadrant & 1) == 1, cosine, sine)
    return jnp.where((quadrant & 2) == 2, -value, value)


def head_mask(rows_per_head):
    shape = (GROUP * rows_per_head, WIDE)
    return iota(shape, 0) // rows_per_head == iota(shape, 1) // HEAD


def split3(x):
    hi = x.astype(BF)
    rest = x - hi.astype(F32)
    mid = rest.astype(BF)
    lo = (rest - mid.astype(F32)).astype(BF)
    return hi, mid, lo


def put_scalars(base, columns):
    lane = iota(base.shape, 1)
    for n, column in enumerate(columns):
        base = jnp.where(lane == BLOCK + n, column.astype(F32), base)
    return base


def stack_slabs(array, group):
    part = array[:, group * WIDE : (group + 1) * WIDE]
    return jnp.concatenate(
        [part[SLAB * (h % RATE) : SLAB * (h % RATE) + SLAB] for h in range(GROUP)], axis=0
    )


def unstack_slabs(stack):
    return jnp.concatenate(
        [
            stack[SLAB * o : SLAB * o + SLAB] + stack[SLAB * (o + RATE) : SLAB * (o + RATE) + SLAB]
            for o in range(RATE)
        ],
        axis=0,
    )


def seg_index():
    return lax.axis_index("xh") * 4 + lax.axis_index("y")


def first_kernel(
    length_ref, coord_ref, cot_ref, tok_ref, w_out_ref, w_qkv_ref,
    message_ref, packed_ref, g_ref, xhat_out, out_grad_out,
):
    length = length_ref[0]
    base = seg_index() * ROWS
    order = regroup()
    coords = coord_ref[0].astype(F32).astype(BF)
    cotangent, tokens, w_out = cot_ref[0], tok_ref[0], w_out_ref[...]
    live = (base + place_of(iota((ROWS, 1), 0))) < length
    out_grad = jnp.where(live, mm(order, cotangent), 0.0).astype(BF)
    out_grad_out.put(out_grad)
    g = mm_nt(out_grad, w_out).astype(BF)
    g_ref[...] = g
    coords = mm_nt(order, coords)
    embedded = mm(order, tokens) + sin_cos_code(coords[:, 0:1], coords[:, 1:2])
    centred = embedded - jnp.mean(embedded, axis=-1, keepdims=True)
    rstd = lax.rsqrt(jnp.mean(centred * centred, axis=-1, keepdims=True) + EPSILON)
    xhat = centred * rstd
    xhat_out.put(jnp.concatenate([xhat, jnp.broadcast_to(rstd, (ROWS, 128))], axis=1))
    packed = mm(xhat.astype(BF), w_qkv_ref[...]).astype(BF)
    packed_ref[...] = packed

    mask = head_mask(SLAB)
    key_col = place_of(iota((1, ROWS), 1))
    row = iota((GROUP * SLAB, 1), 0)
    query_col = RATE * (row % SLAB) + (row // SLAB) % RATE
    allowed = jnp.logical_or(base + key_col < length, key_col == query_col)
    scalars = []
    for group in range(2):
        q = jnp.where(mask, stack_slabs(packed[:, :D], group).astype(F32), 0.0).astype(BF)
        gs = stack_slabs(g, group).astype(F32)
        k = packed[:, D + group * WIDE : D + (group + 1) * WIDE]
        v = packed[:, 2 * D + group * WIDE : 2 * D + (group + 1) * WIDE]
        s = jnp.where(allowed, mm_nt(q, k) * SCALE, NEG_FILL)
        top = jnp.max(s, axis=-1, keepdims=True)
        e = jnp.exp(s - top)
        total = jnp.sum(e, axis=-1, keepdims=True)
        lse = top + jnp.log(total)
        out = mm((e / total).astype(BF), v)
        g_dot = jnp.sum(jnp.where(mask, gs * out, 0.0), axis=-1, keepdims=True)
        scalars.append((lse, g_dot))

    lane = iota((SLAB, BLOCK), 1)
    pad = jnp.zeros((SLAB, 128 - BLOCK), F32)
    for j in range(N_SEG):
        r0 = SLAB * ((2 * j) % RATE)
        columns = [[], []]
        for h in (2 * j, 2 * j + 1):
            at = (h % GROUP) * SLAB
            for which in range(2):
                columns[which] += list(split3(scalars[h // GROUP][which][at : at + SLAB]))
        for a in range(4):
            if a < 3:
                part = packed[r0 : r0 + 2 * SLAB, a * D + BLOCK * j : a * D + BLOCK * (j + 1)]
            else:
                part = g[r0 : r0 + 2 * SLAB, BLOCK * j : BLOCK * (j + 1)]
            part = part.astype(F32)
            part = jnp.where(lane < HEAD, part[:SLAB], part[SLAB:])
            part = jnp.concatenate([part, pad], axis=1)
            if a < 2:
                part = put_scalars(part, columns[a])
            message_ref[j, a] = part.astype(BF)


def by_owner(array, width, padded):
    pad = jnp.zeros((ROWS, padded - 8 * width), array.dtype)
    sides = []
    for c in range(2):
        pieces = []
        for z_hi in range(2):
            for xl in range(2):
                for z_lo in range(4):
                    dp = (z_hi * 4 + z_lo) * 4 + xl * 2 + c
                    pieces.append(array[:, width * dp : width * (dp + 1)])
            pieces.append(pad)
        sides.append(jnp.concatenate(pieces, axis=1).astype(BF))
    first = lax.axis_index("core") == 0
    return jnp.where(first, sides[0], sides[1]), jnp.where(first, sides[1], sides[0])


def dense_kernel(
    length_ref, packed_ref, g_ref, xhat_ref, out_grad_ref,
    back_ref, soft_ref, early_ref,
):
    length = length_ref[0]
    base = seg_index() * ROWS
    mask = head_mask(ROWS)
    row = iota((GROUP * ROWS, 1), 0)
    key_col = place_of(iota((1, ROWS), 1))
    query_col = place_of(row % ROWS)
    allowed = jnp.logical_or(base + key_col < length, key_col == query_col)
    free = (row % ROWS) // SLAB != (row // ROWS) % RATE

    def spread(part):
        return jnp.where(mask, jnp.concatenate([part.astype(F32)] * GROUP, axis=0), 0.0)

    def fold(stack):
        stack = jnp.where(mask, stack, 0.0)
        return sum(stack[ROWS * h : ROWS * (h + 1)] for h in range(GROUP))

    for group in range(2):
        lanes = slice(group * WIDE, (group + 1) * WIDE)
        q = spread(packed_ref[:, group * WIDE : (group + 1) * WIDE]).astype(BF)
        k = packed_ref[:, D + group * WIDE : D + (group + 1) * WIDE]
        v = packed_ref[:, 2 * D + group * WIDE : 2 * D + (group + 1) * WIDE]
        gm = spread(g_ref[:, lanes])
        gb = gm.astype(BF)
        s = jnp.where(allowed, mm_nt(q, k) * SCALE, NEG_FILL)
        e = jnp.exp(s - jnp.max(s, axis=-1, keepdims=True))
        p = e / jnp.sum(e, axis=-1, keepdims=True)
        out = mm(p.astype(BF), v)
        delta = jnp.sum(gm * out, axis=-1, keepdims=True)
        dp = mm_nt(gb, v)
        back_ref[3, :, lanes] = fold(out)
        free_p = jnp.where(free, p, 0.0)
        ds = (free_p * (dp - delta) * SCALE).astype(BF)
        back_ref[0, :, lanes] = fold(mm(ds, k))
        back_ref[1, :, lanes] = mm_tn(ds, q)
        back_ref[2, :, lanes] = mm_tn(free_p.astype(BF), gb)
        for h in range(GROUP):
            at = ROWS * h + SLAB * (h % RATE)
            to = slice(SLAB * h, SLAB * (h + 1))
            soft_ref[group, 0, to] = p[at : at + SLAB]
            soft_ref[group, 1, to] = dp[at : at + SLAB]
    mine, theirs = by_owner(out_grad_ref[...].astype(F32), 24, OUT_HALF)
    early_ref[:, : 2 * OUT_HALF] = theirs
    early_ref[:, 2 * OUT_HALF : 4 * OUT_HALF] = mine
    early_ref[:, 4 * OUT_HALF :] = xhat_ref[:, :D].astype(BF)


def dilated_kernel(length_ref, message_ref, reply_ref):
    length = length_ref[0]
    j = seg_index()
    n = N_SEG * SLAB
    stack = []
    for a in range(4):
        stack.append(jnp.concatenate([message_ref[i, a] for i in range(N_SEG)], axis=0))
    q, k, v, g = stack
    lane = iota((n, 128), 1)
    scalar_lane = q.astype(F32), k.astype(F32)
    key = iota((1, n), 1)
    query = iota((n, 1), 0)
    outs = [jnp.zeros((n, 128), F32) for _ in range(4)]
    columns = [[], []]
    for half in range(2):
        mine = jnp.logical_and(lane >= HEAD * half, lane < HEAD * (half + 1))
        offset = (2 * j + half) % RATE

        def scalar(which):
            at = BLOCK + 3 * half
            x = scalar_lane[which]
            return x[:, at : at + 1] + x[:, at + 1 : at + 2] + x[:, at + 2 : at + 3]

        dense_lse, dense_dot = scalar(0), scalar(1)
        qm = jnp.where(mine, q.astype(F32), 0.0).astype(BF)
        gf = jnp.where(mine, g.astype(F32), 0.0)
        gm = gf.astype(BF)
        allowed = jnp.logical_or(RATE * key + offset < length, key == query)
        s = jnp.where(allowed, mm_nt(qm, k) * SCALE, NEG_FILL)
        top = jnp.max(s, axis=-1, keepdims=True)
        e = jnp.exp(s - top)
        total = jnp.sum(e, axis=-1, keepdims=True)
        lse = top + jnp.log(total)
        p = e / total
        out = mm(p.astype(BF), v)
        larger = jnp.maximum(lse, dense_lse)
        dense_part = jnp.exp(dense_lse - larger)
        own_part = jnp.exp(lse - larger)
        both = dense_part + own_part
        dense_part = dense_part / both
        own_part = own_part / both
        delta = dense_part * dense_dot + own_part * jnp.sum(gf * out, axis=-1, keepdims=True)
        p = p * own_part
        ds = (p * (mm_nt(gm, v) - delta) * SCALE).astype(BF)
        outs[0] = outs[0] + jnp.where(mine, mm(ds, k), 0.0)
        outs[1] = outs[1] + mm_tn(ds, qm)
        outs[2] = outs[2] + mm_tn(p.astype(BF), gm)
        outs[3] = outs[3] + jnp.where(mine, out * own_part, 0.0)
        columns[0] += list(split3(dense_part))
        columns[1] += list(split3(delta))
    outs[0] = put_scalars(outs[0], columns[0])
    outs[1] = put_scalars(outs[1], columns[1])
    for a in range(4):
        result = outs[a].astype(BF)
        for i in range(N_SEG):
            reply_ref[i, a] = result[SLAB * i : SLAB * (i + 1)]


def join_kernel(
    reply_ref, packed_ref, g_ref, soft_ref, back_ref,
    blended_ref, packed_grad_ref, mine_ref, theirs_ref,
):
    small = head_mask(SLAB)
    shape = (ROWS, D)
    sampled = (iota(shape, 1) // HEAD) % RATE == iota(shape, 0) // SLAB

    def placed(a):
        row = jnp.concatenate(
            [reply_ref[j, a].astype(F32)[:, :BLOCK] for j in range(N_SEG)], axis=1
        )
        return jnp.where(sampled, jnp.concatenate([row] * RATE, axis=0), 0.0)

    def scalars(a, group):
        columns = []
        for h in range(GROUP * group, GROUP * (group + 1)):
            x = reply_ref[h // 2, a].astype(F32)
            at = BLOCK + 3 * (h % 2)
            columns.append(x[:, at : at + 1] + x[:, at + 1 : at + 2] + x[:, at + 2 : at + 3])
        return jnp.concatenate(columns, axis=0)

    parts = [[], [], [], []]
    for group in range(2):
        lanes = slice(group * WIDE, (group + 1) * WIDE)
        share, delta = scalars(0, group), scalars(1, group)
        q = jnp.where(small, stack_slabs(packed_ref[:, :D], group).astype(F32), 0.0).astype(BF)
        gm = jnp.where(small, stack_slabs(g_ref[...], group).astype(F32), 0.0).astype(BF)
        k = packed_ref[:, D + group * WIDE : D + (group + 1) * WIDE]
        p = soft_ref[group, 0] * share
        ds = (p * (soft_ref[group, 1] - delta) * SCALE).astype(BF)
        parts[0].append(back_ref[0, :, lanes] + unstack_slabs(jnp.where(small, mm(ds, k), 0.0)))
        parts[1].append(back_ref[1, :, lanes] + mm_tn(ds, q))
        parts[2].append(back_ref[2, :, lanes] + mm_tn(p.astype(BF), gm))
        parts[3].append(unstack_slabs(jnp.where(small, share, 0.0)))
    whole = [jnp.concatenate(part, axis=1) for part in parts]
    out = back_ref[3]
    blended = jnp.where(sampled, whole[3] * out + placed(3), out).astype(BF)
    blended_ref[...] = blended
    theirs_ref[:, 2 * QKV_HALF :] = blended
    grads = []
    for a in range(3):
        grad = (whole[a] + placed(a)).astype(BF)
        packed_grad_ref[:, a * D : (a + 1) * D] = grad
        grads.append(grad.astype(F32))
    grads = jnp.concatenate(grads, axis=1)
    mine, theirs = by_owner(grads, 72, QKV_HALF)
    mine_ref[...] = mine
    theirs_ref[:, : 2 * QKV_HALF] = theirs


def finish_kernel(
    length_ref, blended_ref, w_out_ref, packed_grad_ref, w_qkv_ref, xhat_ref,
    layer_ref, token_grad_ref, done_ref,
):
    length = length_ref[0]
    base = seg_index() * ROWS
    order = regroup()
    live = (base + place_of(iota((ROWS, 1), 0))) < length
    layer = jnp.where(live, mm(blended_ref[...], w_out_ref[...]), 0.0).astype(BF)
    layer_ref[0] = mm_tn(order, layer).astype(BF)
    dn = mm_nt(packed_grad_ref[...], w_qkv_ref[...])
    xhat = xhat_ref[:, :D]
    mean = jnp.mean(dn, axis=-1, keepdims=True)
    slope = jnp.mean(dn * xhat, axis=-1, keepdims=True)
    dx = ((dn - mean - xhat * slope) * xhat_ref[:, D : D + 1]).astype(BF)
    token_grad_ref[0] = mm_tn(order, dx).astype(BF)
    done_ref[...] = jnp.zeros(done_ref.shape, F32)


def weight_kernel(
    half, own_early_ref, early_ref, blended_ref, late_ref, mine_ref, out_ref
):
    xh, xl, y = lax.axis_index("xh"), lax.axis_index("xl"), lax.axis_index("y")
    core = lax.axis_index("core")

    def both(own, other):
        return jnp.concatenate([own, other], axis=0)

    at = half * QKV_HALF
    qkv = mm_tn(
        both(own_early_ref[:, 4 * OUT_HALF :], early_ref[:, 4 * OUT_HALF :]),
        both(mine_ref[:, at : at + 576], late_ref[:, at : at + 576]),
    ).astype(BF)
    at = half * OUT_HALF
    out = mm_tn(
        both(blended_ref[...], late_ref[:, 2 * QKV_HALF :]),
        both(
            own_early_ref[:, 2 * OUT_HALF + at : 2 * OUT_HALF + at + 192],
            early_ref[:, at : at + 192],
        ),
    ).astype(BF)
    for to_xl in range(2):
        total = jnp.concatenate(
            [
                qkv[:, 288 * to_xl : 288 * (to_xl + 1)].astype(F32),
                out[:, BLOCK * to_xl : BLOCK * (to_xl + 1)].astype(F32),
            ],
            axis=1,
        ).astype(BF)
        for s in range(N_SEG):
            x_rel = 2 * ((s // 4 + xh) % 2) + (to_xl + xl) % 2
            y_rel = (s % 4 - y + 4) % 4
            first = jnp.where(core == 1, y_rel, x_rel)
            second = jnp.where(core == 1, x_rel, y_rel)
            out_ref[first, second] = total[BLOCK * s : BLOCK * (s + 1)]


def first_sum_kernel(*refs):
    out_ref = refs[-1]
    for half in range(2):
        own_ref, a_ref, b_ref, c_ref = refs[4 * half : 4 * half + 4]
        for k in range(4):
            total = own_ref[0, k].astype(F32) + a_ref[k].astype(F32)
            total = total + (b_ref[k].astype(F32) + c_ref[k].astype(F32))
            out_ref[k, :, half * WIDE : (half + 1) * WIDE] = total.astype(BF)


def second_sum_kernel(own_ref, a_ref, b_ref, c_ref, out_ref):
    whole = own_ref[0].astype(F32) + a_ref[...].astype(F32)
    whole = whole + (b_ref[...].astype(F32) + c_ref[...].astype(F32))
    for half in range(2):
        total = whole[:, half * WIDE : (half + 1) * WIDE]
        for z in range(4):
            piece = jnp.concatenate(
                [total[:, 72 * z : 72 * z + 72], total[:, 288 + 24 * z : 312 + 24 * z]], axis=1
            )
            side = jnp.concatenate([piece[72:, 32 * n : 32 * n + 32] for n in range(3)], axis=0)
            out_ref[4 * half + z] = jnp.concatenate([piece[:72], side], axis=1).astype(BF)


def last_sum_kernel(parts_ref, in_ref, out_ref):
    total = parts_ref[0].astype(F32)
    for z in range(1, 8):
        total = total + parts_ref[z].astype(F32)
    side = total[:, BLOCK:]
    foot = jnp.concatenate([side[24 * n : 24 * n + 24] for n in range(3)], axis=1)
    total = jnp.concatenate([total[:, :BLOCK], foot], axis=0).T
    in_ref[...] = total[:72]
    out_ref[...] = total[72:]


class Held:
    def __init__(self, source, target, sem):
        self.target = target
        self.copy = pltpu.make_async_copy(source, target, sem)
        self.copy.start()
        self.here = False

    def __getitem__(self, index):
        if not self.here:
            self.copy.wait()
            self.here = True
        return self.target[index]


class Sent:
    def __init__(self, slot, target, sem):
        self.slot = slot
        self.copy = pltpu.make_async_copy(slot, target, sem)

    def put(self, value):
        self.slot[...] = value
        self.copy.start()


def call(kernel, outs, *inputs):
    specs = {"s": SMEM, "v": VMEM, "f": ANY, "h": ANY, "n": ANY}
    kinds = [kind for kind, _ in inputs]
    arrays = [
        pltpu.with_memory_space_constraint(x, pltpu.HBM) if kind == "h" else x
        for kind, x in inputs
    ]
    moved = [x for kind, x in inputs if kind in "fh"]
    moved += [jax.ShapeDtypeStruct(*out[:2]) for out in outs if len(out) > 2]

    def body(*refs):
        n, m = len(kinds), len(outs)
        slots = list(refs[n + m : -1]) if moved else []
        given, sent = [], []
        for kind, ref in zip(kinds, refs[:n]):
            if kind in "fh":
                given.append(Held(ref, slots.pop(0), refs[-1].at[len(slots)]))
            elif kind != "n":
                given.append(ref)
        for out, ref in zip(outs, refs[n : n + m]):
            if len(out) > 2:
                ref = Sent(slots.pop(0), ref, refs[-1].at[len(slots)])
                sent.append(ref)
            given.append(ref)
        kernel(*given)
        for ref in sent:
            ref.copy.wait()

    scratch = [pltpu.VMEM(x.shape, x.dtype) for x in moved]
    if moved:
        scratch.append(pltpu.SemaphoreType.DMA((len(moved),)))
    return pl.pallas_call(
        body,
        out_shape=[
            pltpu.HBM(*out[:2]) if len(out) > 2 else jax.ShapeDtypeStruct(*out) for out in outs
        ],
        in_specs=[specs[kind] for kind in kinds],
        out_specs=[ANY if len(out) > 2 else VMEM for out in outs],
        scratch_shapes=scratch,
        compiler_params=pltpu.CompilerParams(vmem_limit_bytes=LIMIT),
        name=kernel.__name__,
    )(*arrays)


def named(name, kernel):
    def run(*refs):
        kernel(*refs)

    run.__name__ = name
    return run


def to_core(x):
    return lax.ppermute(x, "core", [(0, 1), (1, 0)])


def swap(x, k, stage):
    pairs = []
    for i in range(32):
        xl, core, xh, y = i // 16, (i // 8) % 2, (i // 4) % 2, i % 4
        if core != stage:
            y = (y + k) % 4
        else:
            xl, xh = xl ^ (k % 2), xh ^ (k // 2)
        pairs.append((i, ((xl * 2 + core) * 2 + xh) * 4 + y))
    return lax.ppermute(x, ("xl", "core", "xh", "y"), pairs)


def per_device(tokens, coords, lengths, w_qkv, w_out, cotangent):
    message, packed, g, xhat, out_grad = call(
        first_kernel,
        [
            ((N_SEG, 4, SLAB, 128), BF),
            ((ROWS, 3 * D), BF),
            ((ROWS, D), BF),
            ((ROWS, D + 128), F32, "h"),
            ((ROWS, D), BF, "h"),
        ],
        ("s", lengths),
        ("h", jnp.transpose(coords, (0, 2, 1))),
        ("h", cotangent),
        ("h", tokens),
        ("h", w_out),
        ("h", w_qkv),
    )
    message = lax.all_to_all(message, ("xh", "y"), 0, 0, tiled=True)
    back, soft, own_early = call(
        dense_kernel,
        [
            ((4, ROWS, D), F32),
            ((2, 2, GROUP * SLAB, ROWS), F32),
            ((ROWS, 4 * OUT_HALF + D), BF),
        ],
        ("s", lengths),
        ("v", packed),
        ("v", g),
        ("h", xhat),
        ("h", out_grad),
    )
    (reply,) = call(
        dilated_kernel,
        [((N_SEG, 4, SLAB, 128), BF)],
        ("s", lengths),
        ("v", message),
        ("n", soft),
    )
    reply = lax.all_to_all(reply, ("xh", "y"), 0, 0, tiled=True)
    early = to_core(own_early)
    blended, packed_grad, mine, late = call(
        join_kernel,
        [
            ((ROWS, D), BF),
            ((ROWS, 3 * D), BF),
            ((ROWS, 2 * QKV_HALF), BF),
            ((ROWS, 2 * QKV_HALF + D), BF),
        ],
        ("v", reply),
        ("v", packed),
        ("v", g),
        ("v", soft),
        ("v", back),
        ("n", early),
    )
    late = to_core(late)
    halves = []
    for half in range(2):
        (partial,) = call(
            named("weight_kernel", functools.partial(weight_kernel, half)),
            [((4, 4, BLOCK, WIDE), BF)],
            ("v", own_early),
            ("v", early),
            ("v", blended),
            ("v", late),
            ("v", mine),
        )
        halves.append(partial)
    layer_out, token_grad, done = call(
        finish_kernel,
        [((1, ROWS, D), BF), ((1, ROWS, D), BF), ((8, 128), F32)],
        ("s", lengths),
        ("f", blended),
        ("h", w_out),
        ("f", packed_grad),
        ("h", w_qkv),
        ("h", xhat),
    )
    terms = []
    for partial in halves:
        terms.append(("v", partial))
        terms += [("v", swap(partial[k], k, 0)) for k in (1, 3, 2)]
    (partial,) = call(first_sum_kernel, [((4, BLOCK, D), BF)], *terms, ("n", done))
    terms = [("v", swap(partial[k], k, 1)) for k in (1, 3, 2)]
    (partial,) = call(
        second_sum_kernel, [((8, 72, 128), BF)], ("v", partial), *terms
    )
    arrived = lax.all_to_all(partial, "z", 0, 0, tiled=True)
    grad_in, grad_out = call(
        last_sum_kernel, [((72, BLOCK), F32), ((24, BLOCK), F32)], ("v", arrived)
    )
    return layer_out, token_grad, grad_in.T, grad_out.T


def solution(mesh):
    devices = mesh.devices.reshape(8, 2, 2, 2, 4)
    fine = Mesh(devices, ("z", "xl", "core", "xh", "y"))
    dp, seg = ("z", "xl", "core"), ("xh", "y")
    placed = (P(dp, seg, None), P(dp, seg, None), P(dp), P(), P(), P(dp, seg, None))
    return jax.shard_map(
        per_device,
        mesh=fine,
        in_specs=placed,
        out_specs=(P(dp, seg, None), P(dp, seg, None), P(seg, dp), P(seg, dp)),
        check_vma=False,
    )
```

```python
import functools

import jax
import jax.numpy as jnp
from jax import lax
from jax.experimental import pallas as pl
from jax.experimental.pallas import tpu as pltpu
from jax.sharding import Mesh
from jax.sharding import PartitionSpec as P

HEADS = 16
RATE = 4
HEAD = 48
GROUP = 8
WIDE = GROUP * HEAD
ROWS = 128
SLAB = ROWS // RATE
D = 768
N_SEG = 8
BLOCK = 96
QKV_HALF = 640
OUT_HALF = 256
EPSILON = 1e-05
NEG_FILL = -1e30
SCALE = HEAD ** (-0.5)
BF = jnp.bfloat16
F32 = jnp.float32
VMEM = pl.BlockSpec(memory_space=pltpu.VMEM)
SMEM = pl.BlockSpec(memory_space=pltpu.SMEM)
ANY = pl.BlockSpec(memory_space=pl.ANY)
LIMIT = 20 * 1024 * 1024


def iota(shape, dim):
    return lax.broadcasted_iota(jnp.int32, shape, dim)


def mm(a, b):
    return lax.dot_general(a, b, (((1,), (0,)), ((), ())), preferred_element_type=F32)


def mm_nt(a, b):
    return lax.dot_general(a, b, (((1,), (1,)), ((), ())), preferred_element_type=F32)


def mm_tn(a, b):
    return lax.dot_general(a, b, (((0,), (0,)), ((), ())), preferred_element_type=F32)


def regroup():
    row, col = iota((ROWS, ROWS), 0), iota((ROWS, ROWS), 1)
    return (col == RATE * (row % SLAB) + row // SLAB).astype(BF)


def place_of(row):
    return RATE * (row % SLAB) + row // SLAB


def sin_cos_code(c0, c1):
    quarter = D // 4
    col = iota((1, D), 1)
    block = col // quarter
    freqs = jnp.exp((-jnp.log(F32(10000.0))) * (col - block * quarter).astype(F32) / quarter)
    angle = jnp.where(block < 2, c0, c1) * freqs
    turns = jnp.floor(angle * F32(0.6366197723675814) + F32(0.5))
    rest = angle - turns * F32(1.5703125)
    rest = rest - turns * F32(4.837512969970703e-4)
    rest = rest - turns * F32(7.549789948768648e-8)
    sq = rest * rest
    sine = rest + rest * sq * (
        F32(-1.6666654611e-1) + sq * (F32(8.3321608736e-3) + sq * F32(-1.9515295891e-4))
    )
    cosine = (
        F32(1.0)
        - F32(0.5) * sq
        + sq * sq * (F32(4.166664568298827e-2) + sq * (F32(-1.388731625493765e-3) + sq * F32(2.443315711809948e-5)))
    )
    quadrant = turns.astype(jnp.int32) + (block & 1)
    value = jnp.where((quadrant & 1) == 1, cosine, sine)
    return jnp.where((quadrant & 2) == 2, -value, value)


def head_mask(rows_per_head):
    shape = (GROUP * rows_per_head, WIDE)
    return iota(shape, 0) // rows_per_head == iota(shape, 1) // HEAD


def split3(x):
    hi = x.astype(BF)
    rest = x - hi.astype(F32)
    mid = rest.astype(BF)
    lo = (rest - mid.astype(F32)).astype(BF)
    return hi, mid, lo


def put_scalars(base, columns):
    lane = iota(base.shape, 1)
    for n, column in enumerate(columns):
        base = jnp.where(lane == BLOCK + n, column.astype(F32), base)
    return base


def stack_slabs(array, group):
    part = array[:, group * WIDE : (group + 1) * WIDE]
    return jnp.concatenate(
        [part[SLAB * (h % RATE) : SLAB * (h % RATE) + SLAB] for h in range(GROUP)], axis=0
    )


def unstack_slabs(stack):
    return jnp.concatenate(
        [
            stack[SLAB * o : SLAB * o + SLAB] + stack[SLAB * (o + RATE) : SLAB * (o + RATE) + SLAB]
            for o in range(RATE)
        ],
        axis=0,
    )


def seg_index():
    return lax.axis_index("xh") * 4 + lax.axis_index("y")


def first_kernel(
    length_ref, coord_ref, cot_ref, tok_ref, w_out_ref, w_qkv_ref,
    message_ref, packed_ref, g_ref, xhat_out, out_grad_out,
):
    length = length_ref[0]
    base = seg_index() * ROWS
    order = regroup()
    coords = coord_ref[0].astype(F32).astype(BF)
    cotangent, tokens, w_out = cot_ref[0], tok_ref[0], w_out_ref[...]
    live = (base + place_of(iota((ROWS, 1), 0))) < length
    out_grad = jnp.where(live, mm(order, cotangent), 0.0).astype(BF)
    out_grad_out.put(out_grad)
    g = mm_nt(out_grad, w_out).astype(BF)
    g_ref[...] = g
    coords = mm_nt(order, coords)
    embedded = mm(order, tokens) + sin_cos_code(coords[:, 0:1], coords[:, 1:2])
    centred = embedded - jnp.mean(embedded, axis=-1, keepdims=True)
    rstd = lax.rsqrt(jnp.mean(centred * centred, axis=-1, keepdims=True) + EPSILON)
    xhat = centred * rstd
    xhat_out.put(jnp.concatenate([xhat, jnp.broadcast_to(rstd, (ROWS, 128))], axis=1))
    packed = mm(xhat.astype(BF), w_qkv_ref[...]).astype(BF)
    packed_ref[...] = packed

    mask = head_mask(SLAB)
    key_col = place_of(iota((1, ROWS), 1))
    row = iota((GROUP * SLAB, 1), 0)
    query_col = RATE * (row % SLAB) + (row // SLAB) % RATE
    allowed = jnp.logical_or(base + key_col < length, key_col == query_col)
    scalars = []
    for group in range(2):
        q = jnp.where(mask, stack_slabs(packed[:, :D], group).astype(F32), 0.0).astype(BF)
        gs = stack_slabs(g, group).astype(F32)
        k = packed[:, D + group * WIDE : D + (group + 1) * WIDE]
        v = packed[:, 2 * D + group * WIDE : 2 * D + (group + 1) * WIDE]
        s = jnp.where(allowed, mm_nt(q, k) * SCALE, NEG_FILL)
        top = jnp.max(s, axis=-1, keepdims=True)
        e = jnp.exp(s - top)
        total = jnp.sum(e, axis=-1, keepdims=True)
        lse = top + jnp.log(total)
        out = mm((e / total).astype(BF), v)
        g_dot = jnp.sum(jnp.where(mask, gs * out, 0.0), axis=-1, keepdims=True)
        scalars.append((lse, g_dot))

    lane = iota((SLAB, BLOCK), 1)
    pad = jnp.zeros((SLAB, 128 - BLOCK), F32)
    for j in range(N_SEG):
        r0 = SLAB * ((2 * j) % RATE)
        columns = [[], []]
        for h in (2 * j, 2 * j + 1):
            at = (h % GROUP) * SLAB
            for which in range(2):
                columns[which] += list(split3(scalars[h // GROUP][which][at : at + SLAB]))
        for a in range(4):
            if a < 3:
                part = packed[r0 : r0 + 2 * SLAB, a * D + BLOCK * j : a * D + BLOCK * (j + 1)]
            else:
                part = g[r0 : r0 + 2 * SLAB, BLOCK * j : BLOCK * (j + 1)]
            part = part.astype(F32)
            part = jnp.where(lane < HEAD, part[:SLAB], part[SLAB:])
            part = jnp.concatenate([part, pad], axis=1)
            if a < 2:
                part = put_scalars(part, columns[a])
            message_ref[j, a] = part.astype(BF)


def by_owner(array, width, padded):
    pad = jnp.zeros((ROWS, padded - 8 * width), array.dtype)
    sides = []
    for c in range(2):
        pieces = []
        for z_hi in range(2):
            for xl in range(2):
                for z_lo in range(4):
                    dp = (z_hi * 4 + z_lo) * 4 + xl * 2 + c
                    pieces.append(array[:, width * dp : width * (dp + 1)])
            pieces.append(pad)
        sides.append(jnp.concatenate(pieces, axis=1).astype(BF))
    first = lax.axis_index("core") == 0
    return jnp.where(first, sides[0], sides[1]), jnp.where(first, sides[1], sides[0])


def dense_kernel(
    length_ref, packed_ref, g_ref, xhat_ref, out_grad_ref,
    back_ref, soft_ref, early_ref,
):
    length = length_ref[0]
    base = seg_index() * ROWS
    mask = head_mask(ROWS)
    row = iota((GROUP * ROWS, 1), 0)
    key_col = place_of(iota((1, ROWS), 1))
    query_col = place_of(row % ROWS)
    allowed = jnp.logical_or(base + key_col < length, key_col == query_col)
    free = (row % ROWS) // SLAB != (row // ROWS) % RATE

    def spread(part):
        return jnp.where(mask, jnp.concatenate([part.astype(F32)] * GROUP, axis=0), 0.0)

    def fold(stack):
        stack = jnp.where(mask, stack, 0.0)
        return sum(stack[ROWS * h : ROWS * (h + 1)] for h in range(GROUP))

    for group in range(2):
        lanes = slice(group * WIDE, (group + 1) * WIDE)
        q = spread(packed_ref[:, group * WIDE : (group + 1) * WIDE]).astype(BF)
        k = packed_ref[:, D + group * WIDE : D + (group + 1) * WIDE]
        v = packed_ref[:, 2 * D + group * WIDE : 2 * D + (group + 1) * WIDE]
        gm = spread(g_ref[:, lanes])
        gb = gm.astype(BF)
        s = jnp.where(allowed, mm_nt(q, k) * SCALE, NEG_FILL)
        e = jnp.exp(s - jnp.max(s, axis=-1, keepdims=True))
        p = e / jnp.sum(e, axis=-1, keepdims=True)
        out = mm(p.astype(BF), v)
        delta = jnp.sum(gm * out, axis=-1, keepdims=True)
        dp = mm_nt(gb, v)
        back_ref[3, :, lanes] = fold(out)
        free_p = jnp.where(free, p, 0.0)
        ds = (free_p * (dp - delta) * SCALE).astype(BF)
        back_ref[0, :, lanes] = fold(mm(ds, k))
        back_ref[1, :, lanes] = mm_tn(ds, q)
        back_ref[2, :, lanes] = mm_tn(free_p.astype(BF), gb)
        for h in range(GROUP):
            at = ROWS * h + SLAB * (h % RATE)
            to = slice(SLAB * h, SLAB * (h + 1))
            soft_ref[group, 0, to] = p[at : at + SLAB]
            soft_ref[group, 1, to] = dp[at : at + SLAB]
    mine, theirs = by_owner(out_grad_ref[...].astype(F32), 24, OUT_HALF)
    early_ref[:, : 2 * OUT_HALF] = theirs
    early_ref[:, 2 * OUT_HALF : 4 * OUT_HALF] = mine
    early_ref[:, 4 * OUT_HALF :] = xhat_ref[:, :D].astype(BF)


def dilated_kernel(length_ref, message_ref, reply_ref):
    length = length_ref[0]
    j = seg_index()
    n = N_SEG * SLAB
    stack = []
    for a in range(4):
        stack.append(jnp.concatenate([message_ref[i, a] for i in range(N_SEG)], axis=0))
    q, k, v, g = stack
    lane = iota((n, 128), 1)
    scalar_lane = q.astype(F32), k.astype(F32)
    key = iota((1, n), 1)
    query = iota((n, 1), 0)
    outs = [jnp.zeros((n, 128), F32) for _ in range(4)]
    columns = [[], []]
    for half in range(2):
        mine = jnp.logical_and(lane >= HEAD * half, lane < HEAD * (half + 1))
        offset = (2 * j + half) % RATE

        def scalar(which):
            at = BLOCK + 3 * half
            x = scalar_lane[which]
            return x[:, at : at + 1] + x[:, at + 1 : at + 2] + x[:, at + 2 : at + 3]

        dense_lse, dense_dot = scalar(0), scalar(1)
        qm = jnp.where(mine, q.astype(F32), 0.0).astype(BF)
        gf = jnp.where(mine, g.astype(F32), 0.0)
        gm = gf.astype(BF)
        allowed = jnp.logical_or(RATE * key + offset < length, key == query)
        s = jnp.where(allowed, mm_nt(qm, k) * SCALE, NEG_FILL)
        top = jnp.max(s, axis=-1, keepdims=True)
        e = jnp.exp(s - top)
        total = jnp.sum(e, axis=-1, keepdims=True)
        lse = top + jnp.log(total)
        p = e / total
        out = mm(p.astype(BF), v)
        larger = jnp.maximum(lse, dense_lse)
        dense_part = jnp.exp(dense_lse - larger)
        own_part = jnp.exp(lse - larger)
        both = dense_part + own_part
        dense_part = dense_part / both
        own_part = own_part / both
        delta = dense_part * dense_dot + own_part * jnp.sum(gf * out, axis=-1, keepdims=True)
        p = p * own_part
        ds = (p * (mm_nt(gm, v) - delta) * SCALE).astype(BF)
        outs[0] = outs[0] + jnp.where(mine, mm(ds, k), 0.0)
        outs[1] = outs[1] + mm_tn(ds, qm)
        outs[2] = outs[2] + mm_tn(p.astype(BF), gm)
        outs[3] = outs[3] + jnp.where(mine, out * own_part, 0.0)
        columns[0] += list(split3(dense_part))
        columns[1] += list(split3(delta))
    outs[0] = put_scalars(outs[0], columns[0])
    outs[1] = put_scalars(outs[1], columns[1])
    for a in range(4):
        result = outs[a].astype(BF)
        for i in range(N_SEG):
            reply_ref[i, a] = result[SLAB * i : SLAB * (i + 1)]


def join_kernel(
    reply_ref, packed_ref, g_ref, soft_ref, back_ref,
    blended_ref, packed_grad_ref, mine_ref, theirs_ref,
):
    small = head_mask(SLAB)
    shape = (ROWS, D)
    sampled = (iota(shape, 1) // HEAD) % RATE == iota(shape, 0) // SLAB

    def placed(a):
        row = jnp.concatenate(
            [reply_ref[j, a].astype(F32)[:, :BLOCK] for j in range(N_SEG)], axis=1
        )
        return jnp.where(sampled, jnp.concatenate([row] * RATE, axis=0), 0.0)

    def scalars(a, group):
        columns = []
        for h in range(GROUP * group, GROUP * (group + 1)):
            x = reply_ref[h // 2, a].astype(F32)
            at = BLOCK + 3 * (h % 2)
            columns.append(x[:, at : at + 1] + x[:, at + 1 : at + 2] + x[:, at + 2 : at + 3])
        return jnp.concatenate(columns, axis=0)

    parts = [[], [], [], []]
    for group in range(2):
        lanes = slice(group * WIDE, (group + 1) * WIDE)
        share, delta = scalars(0, group), scalars(1, group)
        q = jnp.where(small, stack_slabs(packed_ref[:, :D], group).astype(F32), 0.0).astype(BF)
        gm = jnp.where(small, stack_slabs(g_ref[...], group).astype(F32), 0.0).astype(BF)
        k = packed_ref[:, D + group * WIDE : D + (group + 1) * WIDE]
        p = soft_ref[group, 0] * share
        ds = (p * (soft_ref[group, 1] - delta) * SCALE).astype(BF)
        parts[0].append(back_ref[0, :, lanes] + unstack_slabs(jnp.where(small, mm(ds, k), 0.0)))
        parts[1].append(back_ref[1, :, lanes] + mm_tn(ds, q))
        parts[2].append(back_ref[2, :, lanes] + mm_tn(p.astype(BF), gm))
        parts[3].append(unstack_slabs(jnp.where(small, share, 0.0)))
    whole = [jnp.concatenate(part, axis=1) for part in parts]
    out = back_ref[3]
    blended = jnp.where(sampled, whole[3] * out + placed(3), out).astype(BF)
    blended_ref[...] = blended
    theirs_ref[:, 2 * QKV_HALF :] = blended
    grads = []
    for a in range(3):
        grad = (whole[a] + placed(a)).astype(BF)
        packed_grad_ref[:, a * D : (a + 1) * D] = grad
        grads.append(grad.astype(F32))
    grads = jnp.concatenate(grads, axis=1)
    mine, theirs = by_owner(grads, 72, QKV_HALF)
    mine_ref[...] = mine
    theirs_ref[:, : 2 * QKV_HALF] = theirs


def finish_kernel(
    length_ref, blended_ref, w_out_ref, packed_grad_ref, w_qkv_ref, xhat_ref,
    layer_ref, token_grad_ref, done_ref,
):
    length = length_ref[0]
    base = seg_index() * ROWS
    order = regroup()
    live = (base + place_of(iota((ROWS, 1), 0))) < length
    layer = jnp.where(live, mm(blended_ref[...], w_out_ref[...]), 0.0).astype(BF)
    layer_ref[0] = mm_tn(order, layer).astype(BF)
    dn = mm_nt(packed_grad_ref[...], w_qkv_ref[...])
    xhat = xhat_ref[:, :D]
    mean = jnp.mean(dn, axis=-1, keepdims=True)
    slope = jnp.mean(dn * xhat, axis=-1, keepdims=True)
    dx = ((dn - mean - xhat * slope) * xhat_ref[:, D : D + 1]).astype(BF)
    token_grad_ref[0] = mm_tn(order, dx).astype(BF)
    done_ref[...] = jnp.zeros(done_ref.shape, F32)


def weight_kernel(
    half, own_early_ref, early_ref, blended_ref, late_ref, mine_ref, out_ref
):
    xh, xl, y = lax.axis_index("xh"), lax.axis_index("xl"), lax.axis_index("y")
    core = lax.axis_index("core")

    def both(own, other):
        return jnp.concatenate([own, other], axis=0)

    at = half * QKV_HALF
    qkv = mm_tn(
        both(own_early_ref[:, 4 * OUT_HALF :], early_ref[:, 4 * OUT_HALF :]),
        both(mine_ref[:, at : at + 576], late_ref[:, at : at + 576]),
    ).astype(BF)
    at = half * OUT_HALF
    out = mm_tn(
        both(blended_ref[...], late_ref[:, 2 * QKV_HALF :]),
        both(
            own_early_ref[:, 2 * OUT_HALF + at : 2 * OUT_HALF + at + 192],
            early_ref[:, at : at + 192],
        ),
    ).astype(BF)
    for to_xl in range(2):
        total = jnp.concatenate(
            [
                qkv[:, 288 * to_xl : 288 * (to_xl + 1)].astype(F32),
                out[:, BLOCK * to_xl : BLOCK * (to_xl + 1)].astype(F32),
            ],
            axis=1,
        ).astype(BF)
        for s in range(N_SEG):
            x_rel = 2 * ((s // 4 + xh) % 2) + (to_xl + xl) % 2
            y_rel = (s % 4 - y + 4) % 4
            first = jnp.where(core == 0, y_rel, x_rel)
            second = jnp.where(core == 0, x_rel, y_rel)
            out_ref[first, second] = total[BLOCK * s : BLOCK * (s + 1)]


def first_sum_kernel(*refs):
    out_ref = refs[-1]
    for half in range(2):
        own_ref, a_ref, b_ref, c_ref = refs[4 * half : 4 * half + 4]
        for k in range(4):
            total = own_ref[0, k].astype(F32) + a_ref[k].astype(F32)
            total = total + (b_ref[k].astype(F32) + c_ref[k].astype(F32))
            out_ref[k, :, half * WIDE : (half + 1) * WIDE] = total.astype(BF)


def second_sum_kernel(own_ref, a_ref, b_ref, c_ref, out_ref):
    whole = own_ref[0].astype(F32) + a_ref[...].astype(F32)
    whole = whole + (b_ref[...].astype(F32) + c_ref[...].astype(F32))
    for half in range(2):
        total = whole[:, half * WIDE : (half + 1) * WIDE]
        for z in range(4):
            piece = jnp.concatenate(
                [total[:, 72 * z : 72 * z + 72], total[:, 288 + 24 * z : 312 + 24 * z]], axis=1
            )
            side = jnp.concatenate([piece[72:, 32 * n : 32 * n + 32] for n in range(3)], axis=0)
            out_ref[4 * half + z] = jnp.concatenate([piece[:72], side], axis=1).astype(BF)


def last_sum_kernel(parts_ref, in_ref, out_ref):
    total = parts_ref[0].astype(F32)
    for z in range(1, 8):
        total = total + parts_ref[z].astype(F32)
    side = total[:, BLOCK:]
    foot = jnp.concatenate([side[24 * n : 24 * n + 24] for n in range(3)], axis=1)
    total = jnp.concatenate([total[:, :BLOCK], foot], axis=0).T
    in_ref[...] = total[:72]
    out_ref[...] = total[72:]


class Held:
    def __init__(self, source, target, sem):
        self.target = target
        self.copy = pltpu.make_async_copy(source, target, sem)
        self.copy.start()
        self.here = False

    def __getitem__(self, index):
        if not self.here:
            self.copy.wait()
            self.here = True
        return self.target[index]


class Sent:
    def __init__(self, slot, target, sem):
        self.slot = slot
        self.copy = pltpu.make_async_copy(slot, target, sem)

    def put(self, value):
        self.slot[...] = value
        self.copy.start()


def call(kernel, outs, *inputs):
    specs = {"s": SMEM, "v": VMEM, "f": ANY, "h": ANY, "n": ANY}
    kinds = [kind for kind, _ in inputs]
    arrays = [
        pltpu.with_memory_space_constraint(x, pltpu.HBM) if kind == "h" else x
        for kind, x in inputs
    ]
    moved = [x for kind, x in inputs if kind in "fh"]
    moved += [jax.ShapeDtypeStruct(*out[:2]) for out in outs if len(out) > 2]

    def body(*refs):
        n, m = len(kinds), len(outs)
        slots = list(refs[n + m : -1]) if moved else []
        given, sent = [], []
        for kind, ref in zip(kinds, refs[:n]):
            if kind in "fh":
                given.append(Held(ref, slots.pop(0), refs[-1].at[len(slots)]))
            elif kind != "n":
                given.append(ref)
        for out, ref in zip(outs, refs[n : n + m]):
            if len(out) > 2:
                ref = Sent(slots.pop(0), ref, refs[-1].at[len(slots)])
                sent.append(ref)
            given.append(ref)
        kernel(*given)
        for ref in sent:
            ref.copy.wait()

    scratch = [pltpu.VMEM(x.shape, x.dtype) for x in moved]
    if moved:
        scratch.append(pltpu.SemaphoreType.DMA((len(moved),)))
    return pl.pallas_call(
        body,
        out_shape=[
            pltpu.HBM(*out[:2]) if len(out) > 2 else jax.ShapeDtypeStruct(*out) for out in outs
        ],
        in_specs=[specs[kind] for kind in kinds],
        out_specs=[ANY if len(out) > 2 else VMEM for out in outs],
        scratch_shapes=scratch,
        compiler_params=pltpu.CompilerParams(vmem_limit_bytes=LIMIT),
        name=kernel.__name__,
    )(*arrays)


def named(name, kernel):
    def run(*refs):
        kernel(*refs)

    run.__name__ = name
    return run


def to_core(x):
    return lax.ppermute(x, "core", [(0, 1), (1, 0)])


def swap(x, k, stage):
    pairs = []
    for i in range(32):
        xl, core, xh, y = i // 16, (i // 8) % 2, (i // 4) % 2, i % 4
        if core == stage:
            y = (y + k) % 4
        else:
            xl, xh = xl ^ (k % 2), xh ^ (k // 2)
        pairs.append((i, ((xl * 2 + core) * 2 + xh) * 4 + y))
    return lax.ppermute(x, ("xl", "core", "xh", "y"), pairs)


def per_device(tokens, coords, lengths, w_qkv, w_out, cotangent):
    message, packed, g, xhat, out_grad = call(
        first_kernel,
        [
            ((N_SEG, 4, SLAB, 128), BF),
            ((ROWS, 3 * D), BF),
            ((ROWS, D), BF),
            ((ROWS, D + 128), F32, "h"),
            ((ROWS, D), BF, "h"),
        ],
        ("s", lengths),
        ("h", jnp.transpose(coords, (0, 2, 1))),
        ("h", cotangent),
        ("h", tokens),
        ("h", w_out),
        ("h", w_qkv),
    )
    message = lax.all_to_all(message, ("xh", "y"), 0, 0, tiled=True)
    back, soft, own_early = call(
        dense_kernel,
        [
            ((4, ROWS, D), F32),
            ((2, 2, GROUP * SLAB, ROWS), F32),
            ((ROWS, 4 * OUT_HALF + D), BF),
        ],
        ("s", lengths),
        ("v", packed),
        ("v", g),
        ("h", xhat),
        ("h", out_grad),
    )
    (reply,) = call(
        dilated_kernel,
        [((N_SEG, 4, SLAB, 128), BF)],
        ("s", lengths),
        ("v", message),
        ("n", soft),
    )
    reply = lax.all_to_all(reply, ("xh", "y"), 0, 0, tiled=True)
    early = to_core(own_early)
    blended, packed_grad, mine, late = call(
        join_kernel,
        [
            ((ROWS, D), BF),
            ((ROWS, 3 * D), BF),
            ((ROWS, 2 * QKV_HALF), BF),
            ((ROWS, 2 * QKV_HALF + D), BF),
        ],
        ("v", reply),
        ("v", packed),
        ("v", g),
        ("v", soft),
        ("v", back),
        ("n", early),
    )
    late = to_core(late)
    halves = []
    for half in range(2):
        (partial,) = call(
            named("weight_kernel", functools.partial(weight_kernel, half)),
            [((4, 4, BLOCK, WIDE), BF)],
            ("v", own_early),
            ("v", early),
            ("v", blended),
            ("v", late),
            ("v", mine),
        )
        halves.append(partial)
    layer_out, token_grad, done = call(
        finish_kernel,
        [((1, ROWS, D), BF), ((1, ROWS, D), BF), ((8, 128), F32)],
        ("s", lengths),
        ("f", blended),
        ("h", w_out),
        ("f", packed_grad),
        ("h", w_qkv),
        ("h", xhat),
    )
    terms = []
    for partial in halves:
        terms.append(("v", partial))
        terms += [("v", swap(partial[k], k, 0)) for k in (1, 3, 2)]
    (partial,) = call(first_sum_kernel, [((4, BLOCK, D), BF)], *terms, ("n", done))
    terms = [("v", swap(partial[k], k, 1)) for k in (3, 1, 2)]
    (partial,) = call(
        second_sum_kernel, [((8, 72, 128), BF)], ("v", partial), *terms
    )
    arrived = lax.all_to_all(partial, "z", 0, 0, tiled=True)
    grad_in, grad_out = call(
        last_sum_kernel, [((72, BLOCK), F32), ((24, BLOCK), F32)], ("v", arrived)
    )
    return layer_out, token_grad, grad_in.T, grad_out.T


def solution(mesh):
    devices = mesh.devices.reshape(8, 2, 2, 2, 4)
    fine = Mesh(devices, ("z", "xl", "core", "xh", "y"))
    dp, seg = ("z", "xl", "core"), ("xh", "y")
    placed = (P(dp, seg, None), P(dp, seg, None), P(dp), P(), P(), P(dp, seg, None))
    return jax.shard_map(
        per_device,
        mesh=fine,
        in_specs=placed,
        out_specs=(P(dp, seg, None), P(dp, seg, None), P(seg, dp), P(seg, dp)),
        check_vma=False,
    )
```
